512 devices in a mesh: shot: 16 (over y, core), tile: 32 (over x, z).
Axes of the slice: x: 4, y: 8, z: 8, core: 2. Of those that a mesh axis runs over, the one named last changes fastest.
Arguments:
- tile_store: int32 [512], replicated, may hold values from 0 to 511, as said below
- apertures: int32 [512, 32], P(('shot', 'tile')), may hold values from 0 to 511, as said below
- model: bfloat16 [512, 2, 4096], P('tile'), may hold values from 0.3984375 to 1.296875
- fwd_states: float32 [512, 2, 64, 16, 128], P(('shot', 'tile')), may hold values from -0.6 to 0.6
- adj_states: float32 [512, 2, 64, 16, 128], P(('shot', 'tile')), may hold values from -0.6 to 0.6
- source_cell: int32 [512], P(('shot', 'tile')), may hold values from 0 to 131071
- wavelet: float32 [512, 8], P(('shot', 'tile')), may hold values from -6 to 6
- receiver_cells: int32 [512, 256], P(('shot', 'tile')), may hold values from 0 to 131071
- residuals: float32 [512, 8, 256], P(('shot', 'tile')), may hold values from -6 to 6
Outputs:
- gradient: float32 [512, 2, 4096], P('tile', None, 'shot')
The draws below stay inside these ranges and needn't reach their ends.
Inputs may be any that keep to these rules, and one draw needn't show every extreme that they name: `tile_store`: A permutation of the tile numbers; the tile in row r of model is held by device r // 16 of tile. `apertures`: each row names 32 distinct tiles; at most 2 of them lie in rows of model held by one device of tile, and in every row some device holds exactly 2 of them.
All inputs are finite; a program needn't handle non-finite values.
Results may differ from the reference program's by a relative error of at most 0.0011.
Values may be sent and summed in bfloat16 or wider, within the bound.
A program may use at most 128 MiB of HBM per device.

```python
import jax
import jax.numpy as jnp
from jax import lax

B = 16
APX = 4
APZ = 8
STEPS = 8
NREC = 256
TPO = 16
AP = 32
CAP = 2
TC = 4096
NX = 64
NY = 16
NZ = 128
CELLS = 131072
SHOTS = 512
TILES = 512
N_SHOT = 16
N_TILE = 32


def owner_layout(key):
    return jax.random.permutation(jax.random.fold_in(key, 11), TILES).astype(jnp.int32)


def draw_tile_store(key, part):
    return owner_layout(key)


def draw_apertures(key, part):
    store = owner_layout(key)
    key = jax.random.fold_in(key, 5)
    inverse = jnp.argsort(store).astype(jnp.int32)

    def slot_perm(slot_key):
        return jax.random.permutation(slot_key, TPO).astype(jnp.int32)

    def draw_shot(shot_key):
        key_owner, key_rest, key_slot, key_order = jax.random.split(shot_key, 4)
        owner_order = jax.random.permutation(key_owner, N_TILE).astype(jnp.int32)
        others = jax.random.permutation(key_rest, (N_TILE - 1) * CAP).astype(jnp.int32)[:AP - CAP]
        owner_index = jnp.concatenate([jnp.zeros((CAP,), jnp.int32), 1 + others // CAP])
        rank_index = jnp.concatenate([jnp.arange(CAP, dtype=jnp.int32), others % CAP])
        owner_ids = owner_order[owner_index]
        slot_table = jax.vmap(slot_perm)(jax.random.split(key_slot, N_TILE))
        slot_ids = slot_table[owner_ids, rank_index]
        tile_ids = inverse[owner_ids * TPO + slot_ids]
        return jax.random.permutation(key_order, tile_ids)
    return jax.vmap(draw_shot)(jax.random.split(key, SHOTS)).astype(jnp.int32)


def with_ends(drawn, stream_key, low, high):
    place = [jax.random.randint(jax.random.fold_in(stream_key, axis), (), 0, length) for axis, length in enumerate(drawn.shape)]
    longest = drawn.shape.index(max(drawn.shape))
    beside = place[:longest] + [(place[longest] + 1) % drawn.shape[longest]] + place[longest + 1:]
    return drawn.at[tuple(place)].set(low).at[tuple(beside)].set(high)


def steps_of(stream_key, shape, cuts, smallest, largest):
    loudness = 1.0
    for axis_at, blocks in cuts:
        heights = jax.random.uniform(jax.random.fold_in(jax.random.fold_in(stream_key, 6), axis_at), (blocks,), jnp.float32, smallest / len(cuts), largest / len(cuts))
        loudness = loudness * jnp.repeat(jnp.exp(heights), shape[axis_at] // blocks).reshape((-1,) + (1,) * (len(shape) - 1 - axis_at))
    return loudness


def noise(key, dims, deviation, most, shards=(), kind=jnp.bfloat16):
    level = steps_of(key, dims, shards, -0.22, 0.18) if shards else 1.0
    result = jax.random.normal(key, dims, jnp.float32) * deviation * level
    return jnp.minimum(jnp.maximum(result, -most), most).astype(kind)


def setup_inputs(seed: int = 0) -> dict:
    streams_of = jax.random.split(jax.random.key(seed), 10)
    return {
        "tile_store": draw_tile_store(jax.random.fold_in(streams_of[9], 71), 0),
        "apertures": draw_apertures(jax.random.fold_in(streams_of[9], 71), 0),
        "model": jnp.clip(0.3984375 + 0.8984375 * jax.random.uniform(streams_of[2], (TILES, 2, TC), jnp.float32) ** steps_of(streams_of[2], (TILES, 2, TC), ((0, 32),), -0.2, 0.2), 0.3984375, 1.296875).astype(jnp.bfloat16),
        "fwd_states": noise(streams_of[3], (SHOTS, 2, NX, NY, NZ), 0.1, 0.6, ((0, 512),), jnp.float32),
        "adj_states": noise(streams_of[4], (SHOTS, 2, NX, NY, NZ), 0.1, 0.6, ((0, 512),), jnp.float32),
        "source_cell": with_ends(jax.random.randint(streams_of[5], (SHOTS,), 0, CELLS), jax.random.fold_in(streams_of[5], 1), 0, CELLS - 1).astype(jnp.int32),
        "wavelet": noise(streams_of[6], (SHOTS, STEPS), 1.0, 6.0, ((0, 512),), jnp.float32),
        "receiver_cells": with_ends(jax.random.randint(streams_of[7], (SHOTS, NREC), 0, CELLS), jax.random.fold_in(streams_of[7], 1), 0, CELLS - 1).astype(jnp.int32),
        "residuals": noise(streams_of[8], (SHOTS, STEPS, NREC), 1.0, 6.0, ((0, 512),), jnp.float32),
    }


COEF_SECOND = (-205.0 / 72.0, 8.0 / 5.0, -1.0 / 5.0, 8.0 / 315.0, -1.0 / 560.0)
COEF_FIRST = (4.0 / 5.0, -1.0 / 5.0, 4.0 / 105.0, -1.0 / 280.0)
SPEED_SCALE = 0.12


def neighbours(wave_field, which_axis):
    extent = wave_field.shape[which_axis]
    pad_spec = [(0, 0), (0, 0), (0, 0)]
    pad_spec[which_axis] = (4, 4)
    padded = jnp.pad(wave_field, pad_spec)
    return [lax.slice_in_dim(padded, 4 + offset, 4 + offset + extent, axis=which_axis) for offset in range(-4, 5)]


def second_sum(wave_field):
    summed = (3.0 * COEF_SECOND[0]) * wave_field
    for which_axis in range(3):
        shifts = neighbours(wave_field, which_axis)
        for reach in range(1, 5):
            summed = summed + COEF_SECOND[reach] * (shifts[4 + reach] + shifts[4 - reach])
    return summed


def first_along(wave_field, which_axis):
    shifts = neighbours(wave_field, which_axis)
    summed = COEF_FIRST[0] * (shifts[5] - shifts[3])
    for reach in range(2, 5):
        summed = summed + COEF_FIRST[reach - 1] * (shifts[4 + reach] - shifts[4 - reach])
    return summed


def operate(wave_field, gain_field, slopes):
    summed = gain_field * second_sum(wave_field)
    for which_axis in range(3):
        summed = summed + slopes[which_axis] * first_along(wave_field, which_axis)
    return summed


def to_volume(tile_block):
    blocks = tile_block.reshape(APX, APZ, 2, B, B, B)
    return blocks.transpose(2, 0, 3, 4, 1, 5).reshape(2, APX * B, B, APZ * B)


def to_tiles(volume):
    blocks = volume.reshape(2, APX, B, B, APZ, B).transpose(1, 4, 0, 2, 3, 5)
    return blocks.reshape(APX * APZ, 2, B * B * B)


def evolve(coeffs, fwd_pair, adj_pair, source_at, pulses, listen_at, traces):
    speed = SPEED_SCALE * coeffs[0]
    gain_field = coeffs[1]
    slopes = [first_along(gain_field, which_axis) for which_axis in range(3)]
    volume_shape = speed.shape

    def inject(wave_field, cells, amounts):
        return wave_field.reshape(-1).at[cells].add(amounts).reshape(volume_shape)

    def forward_step(carry, pulse):
        older, current = carry
        applied = operate(current, gain_field, slopes)
        newer = inject(2.0 * current - older + speed * applied, source_at.reshape(1), pulse.reshape(1))
        return (current, newer), (current, applied)

    unused, (states, images) = lax.scan(forward_step, (fwd_pair[0], fwd_pair[1]), pulses)

    def adjoint_step(carry, inputs):
        later, current, grad_speed, grad_gain = carry
        state, image, listened = inputs
        newer = inject(2.0 * current - later + speed * operate(current, gain_field, slopes), listen_at, listened)
        grad_speed = grad_speed + newer * image
        product = first_along(newer, 0) * first_along(state, 0)
        product = product + first_along(newer, 1) * first_along(state, 1)
        product = product + first_along(newer, 2) * first_along(state, 2)
        grad_gain = grad_gain + speed * product
        return (current, newer, grad_speed, grad_gain), None

    zeros_field = jnp.zeros(volume_shape, jnp.float32)
    final_carry, unused_out = lax.scan(adjoint_step, (adj_pair[0], adj_pair[1], zeros_field, zeros_field), (states, images, traces), reverse=True)
    return jnp.stack([final_carry[2], final_carry[3]])


def reference(tile_store, apertures, model, fwd_states, adj_states, source_cell, wavelet, receiver_cells, residuals):
    def one_shot(wanted, fwd_pair, adj_pair, source_at, pulses, listen_at, traces):
        store_rows = tile_store[wanted]
        coeffs = to_volume(model[store_rows].astype(jnp.float32))
        volume = evolve(coeffs, fwd_pair, adj_pair, source_at, pulses, listen_at, traces)
        return store_rows, to_tiles(volume)

    def group_step(summed, group):
        store_rows, shot_tiles = jax.vmap(one_shot)(*group)
        summed = summed.at[store_rows.reshape(-1)].add(shot_tiles.reshape(-1, 2, TC))
        return summed, None

    inputs = (apertures, fwd_states, adj_states, source_cell, wavelet, receiver_cells, residuals)
    groups = tuple(array.reshape((N_SHOT, N_TILE) + array.shape[1:]) for array in inputs)
    summed, unused = lax.scan(group_step, jnp.zeros((TILES, 2, TC), jnp.float32), groups)
    return summed
```

```python
import jax
import jax.numpy as jnp
import ml_dtypes
import numpy as np
from jax import lax
from jax.experimental import pallas as pl
from jax.experimental.pallas import tpu as pltpu
from jax.sharding import PartitionSpec as P

B = 16
APX = 4
APZ = 8
NX, NY, NZ = 64, 16, 128
STEPS = 8
NREC = 256
COEF_SECOND = (-205.0 / 72.0, 8.0 / 5.0, -1.0 / 5.0, 8.0 / 315.0, -1.0 / 560.0)
COEF_FIRST = (4.0 / 5.0, -1.0 / 5.0, 4.0 / 105.0, -1.0 / 280.0)
SPEED_SCALE = 0.12
F32 = jnp.float32
BF16 = jnp.bfloat16
MESH = pl.DeviceIdType.MESH
PLANES = 16
UNROLL = 4
DEPTH_CHIPS = 8
TURNED = tuple((8 - i) % 8 for i in range(8))


def band(extent, centre):
    second = np.zeros((extent, extent))
    first = np.zeros((extent, extent))
    for to in range(extent):
        second[to, to] = centre
        for reach in range(1, 5):
            if to + reach < extent:
                second[to, to + reach] = COEF_SECOND[reach]
                first[to, to + reach] = COEF_FIRST[reach - 1]
            if to - reach >= 0:
                second[to, to - reach] = COEF_SECOND[reach]
                first[to, to - reach] = -COEF_FIRST[reach - 1]
    return second, first


def parts_of(matrix):
    high = matrix.astype(ml_dtypes.bfloat16)
    low = (matrix - high.astype(np.float64)).astype(ml_dtypes.bfloat16)
    return high, low


def depth_matrix():
    second, first = band(NZ, 3.0 * COEF_SECOND[0])
    high, low = parts_of(np.concatenate([second.T, first.T], axis=1))
    return np.concatenate([high, high, low], axis=0)


def middle_matrix():
    second, first = band(NY, 0.0)
    eight = np.eye(8)
    high, low = parts_of(np.concatenate([np.kron(eight, second), np.kron(eight, first)], axis=0))
    return np.concatenate([high, high, low], axis=1)


def split_two(values):
    high = values.astype(BF16)
    low = (values - high.astype(F32)).astype(BF16)
    return high, low


def turn(block, lane_block):
    block = pltpu.roll(block, 0, 1, stride=B, stride_axis=0)
    for bit in (1, 2, 4):
        block = jnp.where((lane_block & bit) != 0, pltpu.roll(block, 8 - bit, 0), block)
    return pltpu.roll(block, 0, 1, stride=B, stride_axis=0)


def derivatives(window, depth_ref, middle_ref):
    planes = window.shape[0] - 8
    inner = window[4 : 4 + planes].reshape(planes * NY, NZ)
    high, low = split_two(inner)
    along_depth = jnp.dot(
        jnp.concatenate([high, low, high], axis=1), depth_ref[...], preferred_element_type=F32
    )
    halves = range(planes // 8)
    stacked = jnp.concatenate(
        [
            jnp.concatenate([part[128 * h : 128 * h + 128] for h in halves], axis=1)
            for part in (high, low, high)
        ],
        axis=0,
    )
    along_middle = jnp.dot(middle_ref[...], stacked, preferred_element_type=F32)
    middle_second = jnp.concatenate([along_middle[:128, 128 * h : 128 * h + 128] for h in halves], axis=0)
    middle_first = jnp.concatenate([along_middle[128:, 128 * h : 128 * h + 128] for h in halves], axis=0)
    second = along_depth[:, :NZ] + middle_second
    first = None
    for reach in range(1, 5):
        ahead = window[4 + reach : 4 + reach + planes].reshape(planes * NY, NZ)
        behind = window[4 - reach : 4 - reach + planes].reshape(planes * NY, NZ)
        second = second + COEF_SECOND[reach] * (ahead + behind)
        term = COEF_FIRST[reach - 1] * (ahead - behind)
        first = term if first is None else first + term
    return second, first, middle_first, along_depth[:, NZ:]


def wave_kernel(
    tiles_ref, fwd_ref, adj_ref, source_ref, pulse_ref, cells_ref, traces_ref, depth_ref, middle_ref,
    out_ref,
    gain_ref, speed_ref, slope_ref, wave_ref, image_ref, first_ref, inject_ref, hot_ref, sums_ref,
):
    lane_block = lax.broadcasted_iota(jnp.int32, (8, NZ), 1) // B
    rows = PLANES * NY

    def flat(ref, at):
        return ref[pl.ds(at * PLANES, PLANES)].reshape(rows, NZ)

    def put(ref, at, values):
        ref[pl.ds(at * PLANES, PLANES)] = values.reshape(PLANES, NY, NZ)

    border = jnp.zeros((4, NY, NZ), F32)
    for ref in (gain_ref, wave_ref.at[0], wave_ref.at[1]):
        ref[0:4] = border
        ref[NX + 4 : NX + 8] = border

    def unpack(plane, carry):
        for block in range(APX):
            at = block * B + plane
            for field in range(2):
                for half in range(2):
                    lanes = (field * 2 + half) * NZ
                    rows_of = tiles_ref[plane, block * 8 : block * 8 + 8, lanes : lanes + NZ].astype(F32)
                    turned = turn(rows_of, lane_block)
                    if field == 0:
                        speed_ref[at, half * 8 : half * 8 + 8] = SPEED_SCALE * turned
                    else:
                        gain_ref[at + 4, half * 8 : half * 8 + 8] = turned
        return carry

    lax.fori_loop(0, B, unpack, 0)

    def slopes(at, carry):
        window = gain_ref[pl.ds(at * PLANES, PLANES + 8)]
        _, along_x, along_y, along_z = derivatives(window, depth_ref, middle_ref)
        put(slope_ref.at[0], at, along_x)
        put(slope_ref.at[1], at, along_y)
        put(slope_ref.at[2], at, along_z)
        return carry

    lax.fori_loop(0, NX // PLANES, slopes, 0)

    cells = cells_ref[...]
    cell_rows = lax.shift_right_logical(cells, 7)
    cell_lanes = jnp.transpose(jnp.broadcast_to((cells & 127).astype(F32), (8, NREC)))[:, 0:1]
    trace_columns = jnp.transpose(traces_ref[...])
    for at in range(8):
        row_ids = lax.broadcasted_iota(jnp.int32, (128, NREC), 0) + at * 128
        hot_ref[at * 128 : at * 128 + 128] = (row_ids == cell_rows).astype(F32).astype(BF16)
    lane_ids = lax.broadcasted_iota(jnp.int32, (NREC, NZ), 1).astype(F32)
    lane_hot = lane_ids == cell_lanes
    for step in range(STEPS):
        high, low = split_two(jnp.where(lane_hot, trace_columns[:, step : step + 1], 0.0))
        both = jnp.concatenate([high, low], axis=1)
        added = jnp.dot(hot_ref[...], both, preferred_element_type=F32)
        inject_ref[step] = (added[:, :NZ] + added[:, NZ:]).reshape(NX, NY, NZ)

    wave_ref[0, 4 : 4 + NX] = fwd_ref[0]
    wave_ref[1, 4 : 4 + NX] = fwd_ref[1]
    source = source_ref[0]
    source_x, source_y = source // (NY * NZ), (source // NZ) % NY
    source_lane = lax.broadcasted_iota(jnp.int32, (1, NZ), 1) == source % NZ

    def apply(window, at):
        second, along_x, along_y, along_z = derivatives(window, depth_ref, middle_ref)
        applied = flat(gain_ref.at[pl.ds(4, NX)], at) * second
        applied = applied + flat(slope_ref.at[0], at) * along_x
        applied = applied + flat(slope_ref.at[1], at) * along_y
        applied = applied + flat(slope_ref.at[2], at) * along_z
        return applied, along_x, along_y, along_z

    def forward(step, now):
        now_ref, other_ref = wave_ref.at[now], wave_ref.at[1 - now]

        def chunk(at, carry):
            window = now_ref[pl.ds(at * PLANES, PLANES + 8)]
            applied, along_x, along_y, along_z = apply(window, at)
            put(image_ref.at[step], at, applied)
            put(first_ref.at[step, 0], at, along_x)
            put(first_ref.at[step, 1], at, along_y)
            put(first_ref.at[step, 2], at, along_z)
            inner = other_ref.at[pl.ds(4, NX)]
            current = window[4 : 4 + PLANES].reshape(rows, NZ)
            put(inner, at, 2.0 * current - flat(inner, at) + flat(speed_ref, at) * applied)
            return carry

        lax.fori_loop(0, NX // PLANES, chunk, 0, unroll=UNROLL)
        line = other_ref[source_x + 4, pl.ds(source_y, 1)]
        other_ref[source_x + 4, pl.ds(source_y, 1)] = line + jnp.where(source_lane, pulse_ref[0, step], 0.0)

    def forward_pair(pair, carry):
        forward(2 * pair, 1)
        forward(2 * pair + 1, 0)
        return carry

    lax.fori_loop(0, STEPS // 2, forward_pair, 0)

    wave_ref[0, 4 : 4 + NX] = adj_ref[0]
    wave_ref[1, 4 : 4 + NX] = adj_ref[1]

    def backward(step, now, start):
        now_ref, other_ref = wave_ref.at[now], wave_ref.at[1 - now]

        def chunk(at, carry):
            window = now_ref[pl.ds(at * PLANES, PLANES + 8)]
            applied, along_x, along_y, along_z = apply(window, at)
            inner = other_ref.at[pl.ds(4, NX)]
            current = window[4 : 4 + PLANES].reshape(rows, NZ)
            newer = 2.0 * current - flat(inner, at) + flat(speed_ref, at) * applied
            newer = newer + flat(inject_ref.at[step], at)
            put(inner, at, newer)
            speed_part = newer * flat(image_ref.at[step], at)
            if start:
                put(sums_ref.at[0], at, speed_part)
                put(sums_ref.at[1], at, jnp.zeros((rows, NZ), F32))
            else:
                put(sums_ref.at[0], at, flat(sums_ref.at[0], at) + speed_part)
                part = flat(sums_ref.at[1], at) + along_x * flat(first_ref.at[step + 1, 0], at)
                part = part + along_y * flat(first_ref.at[step + 1, 1], at)
                part = part + along_z * flat(first_ref.at[step + 1, 2], at)
                put(sums_ref.at[1], at, part)
            return carry

        lax.fori_loop(0, NX // PLANES, chunk, 0, unroll=UNROLL)

    backward(STEPS - 1, 1, True)

    def backward_pair(pair, carry):
        backward(STEPS - 2 - 2 * pair, 0, False)
        backward(STEPS - 3 - 2 * pair, 1, False)
        return carry

    lax.fori_loop(0, STEPS // 2 - 1, backward_pair, 0)
    backward(0, 0, False)

    def last(at, carry):
        window = wave_ref[1, pl.ds(at * PLANES, PLANES + 8)]
        _, along_x, along_y, along_z = derivatives(window, depth_ref, middle_ref)
        part = flat(sums_ref.at[1], at) + along_x * flat(first_ref.at[0, 0], at)
        part = part + along_y * flat(first_ref.at[0, 1], at)
        part = part + along_z * flat(first_ref.at[0, 2], at)
        put(sums_ref.at[1], at, part * flat(speed_ref, at))
        return carry

    lax.fori_loop(0, NX // PLANES, last, 0, unroll=UNROLL)

    def pack(plane, carry):
        for block in range(APX):
            at = block * B + plane
            for field in range(2):
                for half in range(2):
                    lanes = (field * 2 + half) * NZ
                    values = sums_ref[field, at, half * 8 : half * 8 + 8]
                    out_ref[plane, block * 8 : block * 8 + 8, lanes : lanes + NZ] = turn(values, lane_block)
        return carry

    lax.fori_loop(0, B, pack, 0)


def wave(tiles, fwd, adj, source, pulses, cells, traces):
    vmem = pl.BlockSpec(memory_space=pltpu.VMEM)
    smem = pl.BlockSpec(memory_space=pltpu.SMEM)
    volume = (NX, NY, NZ)
    padded = (NX + 8, NY, NZ)
    return pl.pallas_call(
        wave_kernel,
        out_shape=jax.ShapeDtypeStruct((B, APX * APZ, 4 * NZ), F32),
        in_specs=[vmem, vmem, vmem, smem, smem, vmem, vmem, vmem, vmem],
        out_specs=vmem,
        scratch_shapes=[
            pltpu.VMEM(padded, F32),
            pltpu.VMEM(volume, F32),
            pltpu.VMEM((3,) + volume, F32),
            pltpu.VMEM((2,) + padded, F32),
            pltpu.VMEM((STEPS,) + volume, F32),
            pltpu.VMEM((STEPS, 3) + volume, F32),
            pltpu.VMEM((STEPS,) + volume, F32),
            pltpu.VMEM((NX * NY, NREC), BF16),
            pltpu.VMEM((2,) + volume, F32),
        ],
        compiler_params=pltpu.CompilerParams(vmem_limit_bytes=56 * 1024 * 1024),
        cost_estimate=pl.CostEstimate(flops=10**9, bytes_accessed=5 * 2**20, transcendentals=0),
        name="wave",
    )(tiles, fwd, adj, source, pulses, cells, traces, jnp.asarray(depth_matrix()), jnp.asarray(middle_matrix()))


def place():
    shot, tile = lax.axis_index("shot"), lax.axis_index("tile")
    shots, depths = lax.axis_size("shot"), DEPTH_CHIPS
    across = lax.axis_size("tile") // depths
    return shot, lax.div(tile, depths), lax.rem(tile, depths), shots, across, depths


def shifted(index, by, size):
    return lax.rem(index + by, size)


def greet(shot, x, z, shots, across, depths):
    barrier = pltpu.get_barrier_semaphore()

    def signal(device_id):
        pl.semaphore_signal(barrier, inc=1, device_id=device_id, device_id_type=MESH)

    def to_shot(by, carry):
        signal((shifted(shot, by, shots), x * depths + z))
        return carry

    lax.fori_loop(1, shots, to_shot, 0)
    for by in range(1, across):
        signal((shot, shifted(x, by, across) * depths + z))
    for by in range(1, depths):
        signal((shot, x * depths + shifted(z, by, depths)))
    pl.semaphore_wait(barrier, shots + across + depths - 3)


def remote(src, dst, send_sem, recv_sem, device_id):
    return pltpu.make_async_remote_copy(
        src_ref=src, dst_ref=dst, send_sem=send_sem, recv_sem=recv_sem,
        device_id=device_id, device_id_type=MESH,
    )


def rows_at(start, size):
    return pl.ds(pl.multiple_of(start, size), size)


def fetch_kernel(
    block_ref, names_ref,
    tiles_ref, groups_ref,
    store_ref, pick_ref, names_all, outgoing, incoming,
    z_send, z_recv, x_send, x_recv, name_send, name_recv, shot_send, shot_recv,
):
    shot, x, z, shots, across, depths = place()
    owned = block_ref.shape[0]
    me = x * depths + z
    greet(shot, x, z, shots, across, depths)

    store_ref[rows_at(me * owned, owned)] = block_ref[...]
    names_all[shot] = names_ref[...]

    def z_copy(by):
        return remote(
            block_ref, store_ref.at[rows_at(me * owned, owned)], z_send.at[by], z_recv.at[by],
            (shot, x * depths + shifted(z, by, depths)),
        )

    def name_copy(by):
        return remote(
            names_ref, names_all.at[shot], name_send.at[by], name_recv.at[by],
            (shifted(shot, by, shots), me),
        )

    def x_copy(along, by):
        rows = store_ref.at[rows_at((x * depths + shifted(z, depths - by, depths)) * owned, owned)]
        return remote(
            rows, rows, x_send.at[along, by], x_recv.at[along, by],
            (shot, shifted(x, along, across) * depths + z),
        )

    def start_z(by, carry):
        z_copy(by).start()
        return carry

    def start_name(by, carry):
        name_copy(by).start()
        return carry

    def pass_on(by, carry):
        z_copy(by).wait_recv()
        for along in range(1, across):
            x_copy(along, by).start()
        return carry

    lax.fori_loop(1, depths, start_z, 0)
    for along in range(1, across):
        x_copy(along, 0).start()
    lax.fori_loop(1, shots, start_name, 0)
    lax.fori_loop(1, depths, pass_on, 0)

    def wait_name(by, carry):
        name_copy(by).wait_recv()
        return carry

    lax.fori_loop(1, shots, wait_name, 0)

    group = NZ // (APX * APZ)
    lines, turned = [], []
    for at in range(8):
        if at < shots // group:
            lines.append(sum(names_all[group * at + i, 0:1] for i in range(group)))
            turned.append(sum(names_all[group * at + i, 1:2] for i in range(group)))
        else:
            lines.append(jnp.zeros((1, NZ), F32))
            turned.append(jnp.zeros((1, NZ), F32))
    groups_ref[...] = jnp.concatenate(turned, axis=0)
    columns = jnp.transpose(jnp.concatenate(lines, axis=0))
    total = store_ref.shape[0]
    row_ids = lax.broadcasted_iota(jnp.int32, (NZ, total), 1).astype(F32)
    for at in range(shots // group):
        pick_ref[at] = (row_ids == columns[:, at : at + 1]).astype(F32).astype(BF16)

    def wait_x(by, carry):
        for along in range(1, across):
            x_copy(along, by).wait_recv()
        return carry

    lax.fori_loop(0, depths, wait_x, 0)

    def choose(at, carry):
        chosen = jnp.dot(pick_ref[at], store_ref[...], preferred_element_type=F32).astype(BF16)
        outgoing[pl.ds(at * group, group)] = chosen.reshape(group, APX * APZ, chosen.shape[1])
        return carry

    lax.fori_loop(0, shots // group, choose, 0)

    def shot_copy(by):
        target = shifted(shot, by, shots)
        return remote(
            outgoing.at[target], incoming.at[shot], shot_send.at[by], shot_recv.at[by], (target, me)
        )

    def start_shot(by, carry):
        shot_copy(by).start()
        return carry

    lax.fori_loop(1, shots, start_shot, 0)
    incoming[shot] = outgoing[shot]

    def finish_shot(by, carry):
        shot_copy(by).wait_recv()
        return carry

    lax.fori_loop(1, shots, finish_shot, 0)
    tiles_ref[...] = incoming[...]

    def finish_sends(by, carry):
        shot_copy(by).wait_send()
        name_copy(by).wait_send()
        return carry

    lax.fori_loop(1, shots, finish_sends, 0)

    def finish_z(by, carry):
        z_copy(by).wait_send()
        return carry

    lax.fori_loop(1, depths, finish_z, 0)

    def finish_x(by, carry):
        for along in range(1, across):
            x_copy(along, by).wait_send()
        return carry

    lax.fori_loop(0, depths, finish_x, 0)


def fetch(block, names, shots, tiles):
    vmem = pl.BlockSpec(memory_space=pltpu.VMEM)
    owned, cells = block.shape
    across = tiles // DEPTH_CHIPS
    group = NZ // (APX * APZ)
    dma = pltpu.SemaphoreType.DMA
    return pl.pallas_call(
        fetch_kernel,
        out_shape=(
            jax.ShapeDtypeStruct((shots, APX * APZ, cells), BF16),
            jax.ShapeDtypeStruct((8, NZ), F32),
        ),
        in_specs=[vmem, vmem],
        out_specs=(vmem, vmem),
        scratch_shapes=[
            pltpu.VMEM((tiles * owned, cells), BF16),
            pltpu.VMEM((shots // group, NZ, tiles * owned), BF16),
            pltpu.VMEM((shots, 8, NZ), F32),
            pltpu.VMEM((shots, APX * APZ, cells), BF16),
            pltpu.VMEM((shots, APX * APZ, cells), BF16),
            dma((DEPTH_CHIPS,)), dma((DEPTH_CHIPS,)),
            dma((across, DEPTH_CHIPS)), dma((across, DEPTH_CHIPS)),
            dma((shots,)), dma((shots,)), dma((shots,)), dma((shots,)),
        ],
        compiler_params=pltpu.CompilerParams(
            collective_id=0, has_side_effects=True, vmem_limit_bytes=32 * 1024 * 1024
        ),
        cost_estimate=pl.CostEstimate(flops=3 * 10**8, bytes_accessed=2**21, transcendentals=0),
        name="fetch",
    )(block, names)


def collect_kernel(
    grads_ref, groups_ref,
    out_ref,
    incoming, place_ref, whole, from_x, column, from_z,
    shot_send, shot_recv, x_send, x_recv, z_send, z_recv,
):
    shot, x, z, shots, across, depths = place()
    owned = out_ref.shape[0]
    me = x * depths + z
    greet(shot, x, z, shots, across, depths)

    def shot_copy(by):
        target = shifted(shot, by, shots)
        return remote(
            grads_ref.at[target], incoming.at[shot], shot_send.at[by], shot_recv.at[by], (target, me)
        )

    def start_shot(by, carry):
        shot_copy(by).start()
        return carry

    lax.fori_loop(1, shots, start_shot, 0)
    incoming[shot] = grads_ref[shot]

    group = NZ // (APX * APZ)
    total = whole.shape[0]
    row_ids = lax.broadcasted_iota(jnp.int32, (total, NZ), 0).astype(F32)
    for at in range(shots // group):
        hot = (row_ids == groups_ref[at : at + 1]).astype(F32).astype(BF16)
        place_ref[at, :, :NZ] = hot
        place_ref[at, :, NZ:] = hot

    def finish_shot(by, carry):
        shot_copy(by).wait_recv()
        return carry

    lax.fori_loop(1, shots, finish_shot, 0)

    for at in range(shots // group):
        part = incoming[group * at : group * at + group].reshape(NZ, incoming.shape[2])
        high, low = split_two(part)
        added = jnp.dot(
            place_ref[at], jnp.concatenate([high, low], axis=0), preferred_element_type=F32
        )
        whole[...] = added if at == 0 else whole[...] + added

    def x_copy(along):
        target = shifted(x, along, across)
        return remote(
            whole.at[rows_at(target * depths * owned, depths * owned)], from_x.at[along],
            x_send.at[along], x_recv.at[along], (shot, target * depths + z),
        )

    for along in range(1, across):
        x_copy(along).start()
    for along in range(1, across):
        x_copy(along).wait_recv()
    summed = whole[rows_at(x * depths * owned, depths * owned)]
    for along in range(1, across):
        summed = summed + from_x[along]
    column[...] = summed

    def z_copy(by):
        target = shifted(z, by, depths)
        return remote(
            column.at[rows_at(target * owned, owned)], from_z.at[by],
            z_send.at[by], z_recv.at[by], (shot, x * depths + target),
        )

    for by in range(1, depths):
        z_copy(by).start()
    for by in range(1, depths):
        z_copy(by).wait_recv()
    mine = column[rows_at(z * owned, owned)]
    for by in range(1, depths):
        mine = mine + from_z[by]
    out_ref[...] = mine

    def finish_sends(by, carry):
        shot_copy(by).wait_send()
        return carry

    lax.fori_loop(1, shots, finish_sends, 0)
    for along in range(1, across):
        x_copy(along).wait_send()
    for by in range(1, depths):
        z_copy(by).wait_send()


def collect(grads, groups, tiles, owned):
    vmem = pl.BlockSpec(memory_space=pltpu.VMEM)
    shots, _, cells = grads.shape
    across = tiles // DEPTH_CHIPS
    group = NZ // (APX * APZ)
    dma = pltpu.SemaphoreType.DMA
    return pl.pallas_call(
        collect_kernel,
        out_shape=jax.ShapeDtypeStruct((owned, cells), F32),
        in_specs=[vmem, vmem],
        out_specs=vmem,
        scratch_shapes=[
            pltpu.VMEM((shots, APX * APZ, cells), F32),
            pltpu.VMEM((shots // group, tiles * owned, 2 * NZ), BF16),
            pltpu.VMEM((tiles * owned, cells), F32),
            pltpu.VMEM((across, DEPTH_CHIPS * owned, cells), F32),
            pltpu.VMEM((DEPTH_CHIPS * owned, cells), F32),
            pltpu.VMEM((DEPTH_CHIPS, owned, cells), F32),
            dma((shots,)), dma((shots,)), dma((across,)), dma((across,)),
            dma((DEPTH_CHIPS,)), dma((DEPTH_CHIPS,)),
        ],
        compiler_params=pltpu.CompilerParams(
            collective_id=1, has_side_effects=True, vmem_limit_bytes=32 * 1024 * 1024
        ),
        cost_estimate=pl.CostEstimate(flops=5 * 10**8, bytes_accessed=2**21, transcendentals=0),
        name="collect",
    )(grads, groups)


def per_device(
    tile_store, apertures, model, fwd_states, adj_states, source_cell, wavelet, receiver_cells, residuals
):
    shot = lax.axis_index("shot")
    shots, tiles = lax.axis_size("shot"), lax.axis_size("tile")
    owned = model.shape[0]
    positions = APX * APZ
    cells = model.shape[2] // shots

    rows = tile_store[apertures[0]].astype(F32)
    turned = rows.reshape(APX, APZ)
    turned = jnp.concatenate([turned[:, :1], turned[:, :0:-1]], axis=1).reshape(positions)
    group = NZ // positions
    mine = jnp.repeat(jnp.arange(group) == lax.rem(shot, group), positions)
    lines = [jnp.where(mine, jnp.tile(line, group), 0.0) for line in (rows, turned)]
    names = jnp.concatenate([jnp.stack(lines), jnp.zeros((6, NZ), F32)])

    block = lax.dynamic_slice_in_dim(model, shot * cells, cells, axis=2)
    block = block.reshape(owned, 4, 8, B)
    block = jnp.concatenate([block[:, :, :1], block[:, :, :0:-1]], axis=2).reshape(owned, 2 * cells)

    fetched, groups = fetch(block, names, shots, tiles)
    grads = wave(
        fetched, fwd_states[0], adj_states[0], source_cell, wavelet, receiver_cells, residuals[0]
    )
    return collect(grads, groups, tiles, owned).reshape(owned, 2, cells)


def solution(mesh):
    return jax.shard_map(
        per_device,
        mesh=mesh,
        in_specs=(
            P(),
            P(("shot", "tile"), None),
            P("tile", None, None),
            P(("shot", "tile"), None, None, None, None),
            P(("shot", "tile"), None, None, None, None),
            P(("shot", "tile")),
            P(("shot", "tile"), None),
            P(("shot", "tile"), None),
            P(("shot", "tile"), None, None),
        ),
        out_specs=P("tile", None, "shot"),
        check_vma=False,
    )
```

```python
import jax
import jax.numpy as jnp
import ml_dtypes
import numpy as np
from jax import lax
from jax.experimental import pallas as pl
from jax.experimental.pallas import tpu as pltpu
from jax.sharding import PartitionSpec as P

B = 16
APX = 4
APZ = 8
NX, NY, NZ = 64, 16, 128
STEPS = 8
NREC = 256
COEF_SECOND = (-205.0 / 72.0, 8.0 / 5.0, -1.0 / 5.0, 8.0 / 315.0, -1.0 / 560.0)
COEF_FIRST = (4.0 / 5.0, -1.0 / 5.0, 4.0 / 105.0, -1.0 / 280.0)
SPEED_SCALE = 0.12
F32 = jnp.float32
BF16 = jnp.bfloat16
LEVELS = 32767.0
SMALLEST = 1e-30
MESH = pl.DeviceIdType.MESH
PLANES = 16
UNROLL = 4
DEPTH_CHIPS = 8
TURNED = tuple((8 - i) % 8 for i in range(8))


def band(extent, centre):
    second = np.zeros((extent, extent))
    first = np.zeros((extent, extent))
    for to in range(extent):
        second[to, to] = centre
        for reach in range(1, 5):
            if to + reach < extent:
                second[to, to + reach] = COEF_SECOND[reach]
                first[to, to + reach] = COEF_FIRST[reach - 1]
            if to - reach >= 0:
                second[to, to - reach] = COEF_SECOND[reach]
                first[to, to - reach] = -COEF_FIRST[reach - 1]
    return second, first


def parts_of(matrix):
    high = matrix.astype(ml_dtypes.bfloat16)
    low = (matrix - high.astype(np.float64)).astype(ml_dtypes.bfloat16)
    return high, low


def depth_matrix():
    second, first = band(NZ, 3.0 * COEF_SECOND[0])
    high, low = parts_of(np.concatenate([second.T, first.T], axis=1))
    return np.concatenate([high, high, low], axis=0)


def middle_matrix():
    second, first = band(NY, 0.0)
    eight = np.eye(8)
    high, low = parts_of(np.concatenate([np.kron(eight, second), np.kron(eight, first)], axis=0))
    return np.concatenate([high, high, low], axis=1)


def split_two(values):
    high = values.astype(BF16)
    low = (values - high.astype(F32)).astype(BF16)
    return high, low


def to_levels(values):
    return jnp.round(values).astype(jnp.int32).astype(jnp.int16)


def turn(block, lane_block):
    block = pltpu.roll(block, 0, 1, stride=B, stride_axis=0)
    for bit in (1, 2, 4):
        block = jnp.where((lane_block & bit) != 0, pltpu.roll(block, 8 - bit, 0), block)
    return pltpu.roll(block, 0, 1, stride=B, stride_axis=0)


def derivatives(window, depth_ref, middle_ref):
    planes = window.shape[0] - 8
    inner = window[4 : 4 + planes].reshape(planes * NY, NZ)
    high, low = split_two(inner)
    along_depth = jnp.dot(
        jnp.concatenate([high, low, high], axis=1), depth_ref[...], preferred_element_type=F32
    )
    halves = range(planes // 8)
    stacked = jnp.concatenate(
        [
            jnp.concatenate([part[128 * h : 128 * h + 128] for h in halves], axis=1)
            for part in (high, low, high)
        ],
        axis=0,
    )
    along_middle = jnp.dot(middle_ref[...], stacked, preferred_element_type=F32)
    middle_second = jnp.concatenate([along_middle[:128, 128 * h : 128 * h + 128] for h in halves], axis=0)
    middle_first = jnp.concatenate([along_middle[128:, 128 * h : 128 * h + 128] for h in halves], axis=0)
    second = along_depth[:, :NZ] + middle_second
    first = None
    for reach in range(1, 5):
        ahead = window[4 + reach : 4 + reach + planes].reshape(planes * NY, NZ)
        behind = window[4 - reach : 4 - reach + planes].reshape(planes * NY, NZ)
        second = second + COEF_SECOND[reach] * (ahead + behind)
        term = COEF_FIRST[reach - 1] * (ahead - behind)
        first = term if first is None else first + term
    return second, first, middle_first, along_depth[:, NZ:]


def wave_kernel(
    tiles_ref, fwd_ref, adj_ref, source_ref, pulse_ref, cells_ref, traces_ref, depth_ref, middle_ref,
    out_ref, unit_ref,
    gain_ref, speed_ref, slope_ref, wave_ref, image_ref, first_ref, inject_ref, hot_ref, sums_ref,
):
    lane_block = lax.broadcasted_iota(jnp.int32, (8, NZ), 1) // B
    rows = PLANES * NY

    def flat(ref, at):
        return ref[pl.ds(at * PLANES, PLANES)].reshape(rows, NZ)

    def put(ref, at, values):
        ref[pl.ds(at * PLANES, PLANES)] = values.reshape(PLANES, NY, NZ)

    border = jnp.zeros((4, NY, NZ), F32)
    for ref in (gain_ref, wave_ref.at[0], wave_ref.at[1]):
        ref[0:4] = border
        ref[NX + 4 : NX + 8] = border

    def unpack(plane, carry):
        for block in range(APX):
            at = block * B + plane
            for field in range(2):
                for half in range(2):
                    lanes = (field * 2 + half) * NZ
                    rows_of = tiles_ref[plane, block * 8 : block * 8 + 8, lanes : lanes + NZ].astype(F32)
                    turned = turn(rows_of, lane_block)
                    if field == 0:
                        speed_ref[at, half * 8 : half * 8 + 8] = SPEED_SCALE * turned
                    else:
                        gain_ref[at + 4, half * 8 : half * 8 + 8] = turned
        return carry

    lax.fori_loop(0, B, unpack, 0)

    def slopes(at, carry):
        window = gain_ref[pl.ds(at * PLANES, PLANES + 8)]
        _, along_x, along_y, along_z = derivatives(window, depth_ref, middle_ref)
        put(slope_ref.at[0], at, along_x)
        put(slope_ref.at[1], at, along_y)
        put(slope_ref.at[2], at, along_z)
        return carry

    lax.fori_loop(0, NX // PLANES, slopes, 0)

    cells = cells_ref[...]
    cell_rows = lax.shift_right_logical(cells, 7)
    cell_lanes = jnp.transpose(jnp.broadcast_to((cells & 127).astype(F32), (8, NREC)))[:, 0:1]
    trace_columns = jnp.transpose(traces_ref[...])
    for at in range(8):
        row_ids = lax.broadcasted_iota(jnp.int32, (128, NREC), 0) + at * 128
        hot_ref[at * 128 : at * 128 + 128] = (row_ids == cell_rows).astype(F32).astype(BF16)
    lane_ids = lax.broadcasted_iota(jnp.int32, (NREC, NZ), 1).astype(F32)
    lane_hot = lane_ids == cell_lanes
    for step in range(STEPS):
        high, low = split_two(jnp.where(lane_hot, trace_columns[:, step : step + 1], 0.0))
        both = jnp.concatenate([high, low], axis=1)
        added = jnp.dot(hot_ref[...], both, preferred_element_type=F32)
        inject_ref[step] = (added[:, :NZ] + added[:, NZ:]).reshape(NX, NY, NZ)

    wave_ref[0, 4 : 4 + NX] = fwd_ref[0]
    wave_ref[1, 4 : 4 + NX] = fwd_ref[1]
    source = source_ref[0]
    source_x, source_y = source // (NY * NZ), (source // NZ) % NY
    source_lane = lax.broadcasted_iota(jnp.int32, (1, NZ), 1) == source % NZ

    def apply(window, at):
        second, along_x, along_y, along_z = derivatives(window, depth_ref, middle_ref)
        applied = flat(gain_ref.at[pl.ds(4, NX)], at) * second
        applied = applied + flat(slope_ref.at[0], at) * along_x
        applied = applied + flat(slope_ref.at[1], at) * along_y
        applied = applied + flat(slope_ref.at[2], at) * along_z
        return applied, along_x, along_y, along_z

    def forward(step, now):
        now_ref, other_ref = wave_ref.at[now], wave_ref.at[1 - now]

        def chunk(at, carry):
            window = now_ref[pl.ds(at * PLANES, PLANES + 8)]
            applied, along_x, along_y, along_z = apply(window, at)
            put(image_ref.at[step], at, applied)
            put(first_ref.at[step, 0], at, along_x)
            put(first_ref.at[step, 1], at, along_y)
            put(first_ref.at[step, 2], at, along_z)
            inner = other_ref.at[pl.ds(4, NX)]
            current = window[4 : 4 + PLANES].reshape(rows, NZ)
            put(inner, at, 2.0 * current - flat(inner, at) + flat(speed_ref, at) * applied)
            return carry

        lax.fori_loop(0, NX // PLANES, chunk, 0, unroll=UNROLL)
        line = other_ref[source_x + 4, pl.ds(source_y, 1)]
        other_ref[source_x + 4, pl.ds(source_y, 1)] = line + jnp.where(source_lane, pulse_ref[0, step], 0.0)

    def forward_pair(pair, carry):
        forward(2 * pair, 1)
        forward(2 * pair + 1, 0)
        return carry

    lax.fori_loop(0, STEPS // 2, forward_pair, 0)

    wave_ref[0, 4 : 4 + NX] = adj_ref[0]
    wave_ref[1, 4 : 4 + NX] = adj_ref[1]

    def backward(step, now, start):
        now_ref, other_ref = wave_ref.at[now], wave_ref.at[1 - now]

        def chunk(at, carry):
            window = now_ref[pl.ds(at * PLANES, PLANES + 8)]
            applied, along_x, along_y, along_z = apply(window, at)
            inner = other_ref.at[pl.ds(4, NX)]
            current = window[4 : 4 + PLANES].reshape(rows, NZ)
            newer = 2.0 * current - flat(inner, at) + flat(speed_ref, at) * applied
            newer = newer + flat(inject_ref.at[step], at)
            put(inner, at, newer)
            speed_part = newer * flat(image_ref.at[step], at)
            if start:
                put(sums_ref.at[0], at, speed_part)
                put(sums_ref.at[1], at, jnp.zeros((rows, NZ), F32))
            else:
                put(sums_ref.at[0], at, flat(sums_ref.at[0], at) + speed_part)
                part = flat(sums_ref.at[1], at) + along_x * flat(first_ref.at[step + 1, 0], at)
                part = part + along_y * flat(first_ref.at[step + 1, 1], at)
                part = part + along_z * flat(first_ref.at[step + 1, 2], at)
                put(sums_ref.at[1], at, part)
            return carry

        lax.fori_loop(0, NX // PLANES, chunk, 0, unroll=UNROLL)

    backward(STEPS - 1, 1, True)

    def backward_pair(pair, carry):
        backward(STEPS - 2 - 2 * pair, 0, False)
        backward(STEPS - 3 - 2 * pair, 1, False)
        return carry

    lax.fori_loop(0, STEPS // 2 - 1, backward_pair, 0)
    backward(0, 0, False)

    def last(at, carry):
        window = wave_ref[1, pl.ds(at * PLANES, PLANES + 8)]
        _, along_x, along_y, along_z = derivatives(window, depth_ref, middle_ref)
        part = flat(sums_ref.at[1], at) + along_x * flat(first_ref.at[0, 0], at)
        part = part + along_y * flat(first_ref.at[0, 1], at)
        part = part + along_z * flat(first_ref.at[0, 2], at)
        put(sums_ref.at[1], at, part * flat(speed_ref, at))
        return carry

    lax.fori_loop(0, NX // PLANES, last, 0, unroll=UNROLL)

    def pack(plane, carry):
        for field in range(2):
            for pair in range(APX // 2):
                coded = [[], []]
                for block in (2 * pair, 2 * pair + 1):
                    at = block * B + plane
                    values = [sums_ref[field, at, half * 8 : half * 8 + 8] for half in range(2)]
                    largest = jnp.maximum(jnp.abs(values[0]), jnp.abs(values[1]))
                    largest = jnp.maximum(jnp.max(largest, axis=(0, 1), keepdims=True), SMALLEST)
                    unit_ref[plane, field * APX + block : field * APX + block + 1] = (
                        jnp.broadcast_to(largest * (1.0 / LEVELS), (1, NZ))
                    )
                    levels = LEVELS / largest
                    for half in range(2):
                        coded[half].append(turn(values[half] * levels, lane_block))
                for half in range(2):
                    lanes = (field * 2 + half) * NZ
                    out_ref[plane, pair * 16 : pair * 16 + 16, lanes : lanes + NZ] = to_levels(
                        jnp.concatenate(coded[half], axis=0)
                    )
        return carry

    lax.fori_loop(0, B, pack, 0)


def wave(tiles, fwd, adj, source, pulses, cells, traces):
    vmem = pl.BlockSpec(memory_space=pltpu.VMEM)
    smem = pl.BlockSpec(memory_space=pltpu.SMEM)
    volume = (NX, NY, NZ)
    padded = (NX + 8, NY, NZ)
    return pl.pallas_call(
        wave_kernel,
        out_shape=(
            jax.ShapeDtypeStruct((B, APX * APZ, 4 * NZ), jnp.int16),
            jax.ShapeDtypeStruct((B, 8, NZ), F32),
        ),
        in_specs=[vmem, vmem, vmem, smem, smem, vmem, vmem, vmem, vmem],
        out_specs=(vmem, vmem),
        scratch_shapes=[
            pltpu.VMEM(padded, F32),
            pltpu.VMEM(volume, F32),
            pltpu.VMEM((3,) + volume, F32),
            pltpu.VMEM((2,) + padded, F32),
            pltpu.VMEM((STEPS,) + volume, F32),
            pltpu.VMEM((STEPS, 3) + volume, F32),
            pltpu.VMEM((STEPS,) + volume, F32),
            pltpu.VMEM((NX * NY, NREC), BF16),
            pltpu.VMEM((2,) + volume, F32),
        ],
        compiler_params=pltpu.CompilerParams(vmem_limit_bytes=56 * 1024 * 1024),
        cost_estimate=pl.CostEstimate(flops=10**9, bytes_accessed=5 * 2**20, transcendentals=0),
        name="wave",
    )(tiles, fwd, adj, source, pulses, cells, traces, jnp.asarray(depth_matrix()), jnp.asarray(middle_matrix()))


def place():
    shot, tile = lax.axis_index("shot"), lax.axis_index("tile")
    shots, depths = lax.axis_size("shot"), DEPTH_CHIPS
    across = lax.axis_size("tile") // depths
    return shot, lax.div(tile, depths), lax.rem(tile, depths), shots, across, depths


def shifted(index, by, size):
    return lax.rem(index + by, size)


def greet(shot, x, z, shots, across, depths):
    barrier = pltpu.get_barrier_semaphore()

    def signal(device_id):
        pl.semaphore_signal(barrier, inc=1, device_id=device_id, device_id_type=MESH)

    def to_shot(by, carry):
        signal((shifted(shot, by, shots), x * depths + z))
        return carry

    lax.fori_loop(1, shots, to_shot, 0)
    for by in range(1, across):
        signal((shot, shifted(x, by, across) * depths + z))
    for by in range(1, depths):
        signal((shot, x * depths + shifted(z, by, depths)))
    pl.semaphore_wait(barrier, shots + across + depths - 3)


def remote(src, dst, send_sem, recv_sem, device_id):
    return pltpu.make_async_remote_copy(
        src_ref=src, dst_ref=dst, send_sem=send_sem, recv_sem=recv_sem,
        device_id=device_id, device_id_type=MESH,
    )


def rows_at(start, size):
    return pl.ds(pl.multiple_of(start, size), size)


def fetch_kernel(
    block_ref, names_ref,
    tiles_ref, groups_ref,
    store_ref, pick_ref, names_all, outgoing, incoming,
    z_send, z_recv, x_send, x_recv, name_send, name_recv, shot_send, shot_recv,
):
    shot, x, z, shots, across, depths = place()
    owned = block_ref.shape[0]
    me = x * depths + z
    greet(shot, x, z, shots, across, depths)

    store_ref[rows_at(me * owned, owned)] = block_ref[...]
    names_all[shot] = names_ref[...]

    def z_copy(by):
        return remote(
            block_ref, store_ref.at[rows_at(me * owned, owned)], z_send.at[by], z_recv.at[by],
            (shot, x * depths + shifted(z, by, depths)),
        )

    def name_copy(by):
        return remote(
            names_ref, names_all.at[shot], name_send.at[by], name_recv.at[by],
            (shifted(shot, by, shots), me),
        )

    def x_copy(along, by):
        rows = store_ref.at[rows_at((x * depths + shifted(z, depths - by, depths)) * owned, owned)]
        return remote(
            rows, rows, x_send.at[along, by], x_recv.at[along, by],
            (shot, shifted(x, along, across) * depths + z),
        )

    def start_z(by, carry):
        z_copy(by).start()
        return carry

    def start_name(by, carry):
        name_copy(by).start()
        return carry

    def pass_on(by, carry):
        z_copy(by).wait_recv()
        for along in range(1, across):
            x_copy(along, by).start()
        return carry

    lax.fori_loop(1, depths, start_z, 0)
    for along in range(1, across):
        x_copy(along, 0).start()
    lax.fori_loop(1, shots, start_name, 0)
    lax.fori_loop(1, depths, pass_on, 0)

    def wait_name(by, carry):
        name_copy(by).wait_recv()
        return carry

    lax.fori_loop(1, shots, wait_name, 0)

    group = NZ // (APX * APZ)
    lines, turned = [], []
    for at in range(8):
        if at < shots // group:
            lines.append(sum(names_all[group * at + i, 0:1] for i in range(group)))
            turned.append(sum(names_all[group * at + i, 1:2] for i in range(group)))
        else:
            lines.append(jnp.zeros((1, NZ), F32))
            turned.append(jnp.zeros((1, NZ), F32))
    groups_ref[...] = jnp.concatenate(turned, axis=0)
    columns = jnp.transpose(jnp.concatenate(lines, axis=0))
    total = store_ref.shape[0]
    row_ids = lax.broadcasted_iota(jnp.int32, (NZ, total), 1).astype(F32)
    for at in range(shots // group):
        pick_ref[at] = (row_ids == columns[:, at : at + 1]).astype(F32).astype(BF16)

    def wait_x(by, carry):
        for along in range(1, across):
            x_copy(along, by).wait_recv()
        return carry

    lax.fori_loop(0, depths, wait_x, 0)

    def choose(at, carry):
        chosen = jnp.dot(pick_ref[at], store_ref[...], preferred_element_type=F32).astype(BF16)
        outgoing[pl.ds(at * group, group)] = chosen.reshape(group, APX * APZ, chosen.shape[1])
        return carry

    lax.fori_loop(0, shots // group, choose, 0)

    def shot_copy(by):
        target = shifted(shot, by, shots)
        return remote(
            outgoing.at[target], incoming.at[shot], shot_send.at[by], shot_recv.at[by], (target, me)
        )

    def start_shot(by, carry):
        shot_copy(by).start()
        return carry

    lax.fori_loop(1, shots, start_shot, 0)
    incoming[shot] = outgoing[shot]

    def finish_shot(by, carry):
        shot_copy(by).wait_recv()
        return carry

    lax.fori_loop(1, shots, finish_shot, 0)
    tiles_ref[...] = incoming[...]

    def finish_sends(by, carry):
        shot_copy(by).wait_send()
        name_copy(by).wait_send()
        return carry

    lax.fori_loop(1, shots, finish_sends, 0)

    def finish_z(by, carry):
        z_copy(by).wait_send()
        return carry

    lax.fori_loop(1, depths, finish_z, 0)

    def finish_x(by, carry):
        for along in range(1, across):
            x_copy(along, by).wait_send()
        return carry

    lax.fori_loop(0, depths, finish_x, 0)


def fetch(block, names, shots, tiles):
    vmem = pl.BlockSpec(memory_space=pltpu.VMEM)
    owned, cells = block.shape
    across = tiles // DEPTH_CHIPS
    group = NZ // (APX * APZ)
    dma = pltpu.SemaphoreType.DMA
    return pl.pallas_call(
        fetch_kernel,
        out_shape=(
            jax.ShapeDtypeStruct((shots, APX * APZ, cells), BF16),
            jax.ShapeDtypeStruct((8, NZ), F32),
        ),
        in_specs=[vmem, vmem],
        out_specs=(vmem, vmem),
        scratch_shapes=[
            pltpu.VMEM((tiles * owned, cells), BF16),
            pltpu.VMEM((shots // group, NZ, tiles * owned), BF16),
            pltpu.VMEM((shots, 8, NZ), F32),
            pltpu.VMEM((shots, APX * APZ, cells), BF16),
            pltpu.VMEM((shots, APX * APZ, cells), BF16),
            dma((DEPTH_CHIPS,)), dma((DEPTH_CHIPS,)),
            dma((across, DEPTH_CHIPS)), dma((across, DEPTH_CHIPS)),
            dma((shots,)), dma((shots,)), dma((shots,)), dma((shots,)),
        ],
        compiler_params=pltpu.CompilerParams(
            collective_id=0, has_side_effects=True, vmem_limit_bytes=32 * 1024 * 1024
        ),
        cost_estimate=pl.CostEstimate(flops=3 * 10**8, bytes_accessed=2**21, transcendentals=0),
        name="fetch",
    )(block, names)


def row_levels(values):
    rows, lanes = values.shape
    field = lanes // 2
    units, coded = [], []
    for at in range(2):
        part = values[:, at * field : (at + 1) * field]
        largest = jnp.maximum(jnp.max(jnp.abs(part), axis=1, keepdims=True), SMALLEST)
        units.append(largest * (1.0 / LEVELS))
        coded.append(part * (LEVELS / largest))
    first = lax.broadcasted_iota(jnp.int32, (rows, NZ), 1) == 0
    lines = jnp.transpose(jnp.where(first, units[0], units[1]))[:8]
    return to_levels(jnp.concatenate(coded, axis=1)), lines


def from_levels(levels, units):
    field = levels.shape[1] // 2
    values = levels.astype(F32)
    return jnp.concatenate(
        [values[:, :field] * units[:, 0:1], values[:, field:] * units[:, 1:2]], axis=1
    )


def collect_kernel(
    grads_ref, units_ref, groups_ref,
    out_ref,
    incoming, units_all, place_ref, whole, whole_levels, whole_lines, from_x, lines_x,
    column, column_levels, column_lines, from_z, lines_z, turned_units,
    shot_send, shot_recv, unit_send, unit_recv, x_send, x_recv, xu_send, xu_recv,
    z_send, z_recv, zu_send, zu_recv,
):
    shot, x, z, shots, across, depths = place()
    owned = out_ref.shape[0]
    me = x * depths + z
    greet(shot, x, z, shots, across, depths)

    def shot_copy(by):
        target = shifted(shot, by, shots)
        return remote(
            grads_ref.at[target], incoming.at[shot], shot_send.at[by], shot_recv.at[by], (target, me)
        )

    def unit_copy(by):
        target = shifted(shot, by, shots)
        return remote(
            units_ref.at[target], units_all.at[shot], unit_send.at[by], unit_recv.at[by], (target, me)
        )

    def start_shot(by, carry):
        shot_copy(by).start()
        unit_copy(by).start()
        return carry

    lax.fori_loop(1, shots, start_shot, 0)
    incoming[shot] = grads_ref[shot]
    units_all[shot] = units_ref[shot]

    group = NZ // (APX * APZ)
    total = whole.shape[0]
    row_ids = lax.broadcasted_iota(jnp.int32, (total, NZ), 0).astype(F32)
    for at in range(shots // group):
        hot = (row_ids == groups_ref[at : at + 1]).astype(F32).astype(BF16)
        place_ref[at, :, :NZ] = hot
        place_ref[at, :, NZ:] = hot

    def finish_shot(by, carry):
        shot_copy(by).wait_recv()
        unit_copy(by).wait_recv()
        return carry

    lax.fori_loop(1, shots, finish_shot, 0)

    for at in range(shots // group):
        parts = []
        for member in range(group * at, group * at + group):
            levels = incoming[member].astype(F32)
            for block in range(APX):
                rows = levels[8 * block : 8 * block + 8]
                parts.append(
                    jnp.concatenate(
                        [
                            rows[:, lanes * NZ : lanes * NZ + NZ]
                            * units_all[member, (lanes // 2) * APX + block : (lanes // 2) * APX + block + 1]
                            for lanes in range(4)
                        ],
                        axis=1,
                    )
                )
        high, low = split_two(jnp.concatenate(parts, axis=0))
        added = jnp.dot(
            place_ref[at], jnp.concatenate([high, low], axis=0), preferred_element_type=F32
        )
        whole[...] = added if at == 0 else whole[...] + added

    block = depths * owned
    for at in range(across):
        coded, lines = row_levels(whole[at * block : (at + 1) * block])
        whole_levels[at * block : (at + 1) * block] = coded
        whole_lines[at] = lines

    def x_copy(along):
        target = shifted(x, along, across)
        return remote(
            whole_levels.at[rows_at(target * block, block)], from_x.at[along],
            x_send.at[along], x_recv.at[along], (shot, target * depths + z),
        )

    def x_lines(along):
        target = shifted(x, along, across)
        return remote(
            whole_lines.at[target], lines_x.at[along],
            xu_send.at[along], xu_recv.at[along], (shot, target * depths + z),
        )

    for along in range(1, across):
        x_copy(along).start()
        x_lines(along).start()
    summed = whole[rows_at(x * block, block)]
    for along in range(1, across):
        x_copy(along).wait_recv()
        x_lines(along).wait_recv()
        summed = summed + from_levels(from_x[along], jnp.transpose(lines_x[along]))
    column[...] = summed
    coded, lines = row_levels(summed)
    column_levels[...] = coded
    column_lines[...] = lines

    def z_copy(by):
        target = shifted(z, by, depths)
        return remote(
            column_levels.at[rows_at(target * owned, owned)], from_z.at[by],
            z_send.at[by], z_recv.at[by], (shot, x * depths + target),
        )

    def z_lines(by):
        target = shifted(z, by, depths)
        return remote(
            column_lines, lines_z.at[by], zu_send.at[by], zu_recv.at[by], (shot, x * depths + target)
        )

    for by in range(1, depths):
        z_copy(by).start()
        z_lines(by).start()
    mine = column[rows_at(z * owned, owned)]
    for by in range(1, depths):
        z_copy(by).wait_recv()
        z_lines(by).wait_recv()
        turned_units[by] = jnp.transpose(lines_z[by])
        mine = mine + from_levels(from_z[by], turned_units[by, rows_at(z * owned, owned)])
    out_ref[...] = mine

    def finish_sends(by, carry):
        shot_copy(by).wait_send()
        unit_copy(by).wait_send()
        return carry

    lax.fori_loop(1, shots, finish_sends, 0)
    for along in range(1, across):
        x_copy(along).wait_send()
        x_lines(along).wait_send()
    for by in range(1, depths):
        z_copy(by).wait_send()
        z_lines(by).wait_send()


def collect(grads, units, groups, tiles, owned):
    vmem = pl.BlockSpec(memory_space=pltpu.VMEM)
    shots, _, cells = grads.shape
    depths = DEPTH_CHIPS
    across = tiles // depths
    block = depths * owned
    group = NZ // (APX * APZ)
    dma = pltpu.SemaphoreType.DMA
    int16 = jnp.int16
    return pl.pallas_call(
        collect_kernel,
        out_shape=jax.ShapeDtypeStruct((owned, cells), F32),
        in_specs=[vmem, vmem, vmem],
        out_specs=vmem,
        scratch_shapes=[
            pltpu.VMEM((shots, APX * APZ, cells), int16),
            pltpu.VMEM((shots, 8, NZ), F32),
            pltpu.VMEM((shots // group, tiles * owned, 2 * NZ), BF16),
            pltpu.VMEM((tiles * owned, cells), F32),
            pltpu.VMEM((tiles * owned, cells), int16),
            pltpu.VMEM((across, 8, block), F32),
            pltpu.VMEM((across, block, cells), int16),
            pltpu.VMEM((across, 8, block), F32),
            pltpu.VMEM((block, cells), F32),
            pltpu.VMEM((block, cells), int16),
            pltpu.VMEM((8, block), F32),
            pltpu.VMEM((depths, owned, cells), int16),
            pltpu.VMEM((depths, 8, block), F32),
            pltpu.VMEM((depths, block, 8), F32),
            dma((shots,)), dma((shots,)), dma((shots,)), dma((shots,)),
            dma((across,)), dma((across,)), dma((across,)), dma((across,)),
            dma((depths,)), dma((depths,)), dma((depths,)), dma((depths,)),
        ],
        compiler_params=pltpu.CompilerParams(
            collective_id=1, has_side_effects=True, vmem_limit_bytes=32 * 1024 * 1024
        ),
        cost_estimate=pl.CostEstimate(flops=5 * 10**8, bytes_accessed=2**21, transcendentals=0),
        name="collect",
    )(grads, units, groups)


def per_device(
    tile_store, apertures, model, fwd_states, adj_states, source_cell, wavelet, receiver_cells, residuals
):
    shot = lax.axis_index("shot")
    shots, tiles = lax.axis_size("shot"), lax.axis_size("tile")
    owned = model.shape[0]
    positions = APX * APZ
    cells = model.shape[2] // shots

    rows = tile_store[apertures[0]].astype(F32)
    turned = rows.reshape(APX, APZ)
    turned = jnp.concatenate([turned[:, :1], turned[:, :0:-1]], axis=1).reshape(positions)
    group = NZ // positions
    mine = jnp.repeat(jnp.arange(group) == lax.rem(shot, group), positions)
    lines = [jnp.where(mine, jnp.tile(line, group), 0.0) for line in (rows, turned)]
    names = jnp.concatenate([jnp.stack(lines), jnp.zeros((6, NZ), F32)])

    block = lax.dynamic_slice_in_dim(model, shot * cells, cells, axis=2)
    block = block.reshape(owned, 4, 8, B)
    block = jnp.concatenate([block[:, :, :1], block[:, :, :0:-1]], axis=2).reshape(owned, 2 * cells)

    fetched, groups = fetch(block, names, shots, tiles)
    grads, units = wave(
        fetched, fwd_states[0], adj_states[0], source_cell, wavelet, receiver_cells, residuals[0]
    )
    return collect(grads, units, groups, tiles, owned).reshape(owned, 2, cells)


def solution(mesh):
    return jax.shard_map(
        per_device,
        mesh=mesh,
        in_specs=(
            P(),
            P(("shot", "tile"), None),
            P("tile", None, None),
            P(("shot", "tile"), None, None, None, None),
            P(("shot", "tile"), None, None, None, None),
            P(("shot", "tile")),
            P(("shot", "tile"), None),
            P(("shot", "tile"), None),
            P(("shot", "tile"), None, None),
        ),
        out_specs=P("tile", None, "shot"),
        check_vma=False,
    )
```

```python
import jax
import jax.numpy as jnp
import ml_dtypes
import numpy as np
from jax import lax
from jax.experimental import pallas as pl
from jax.experimental.pallas import tpu as pltpu
from jax.sharding import PartitionSpec as P

B = 16
APX = 4
APZ = 8
NX, NY, NZ = 64, 16, 128
STEPS = 8
NREC = 256
COEF_SECOND = (-205.0 / 72.0, 8.0 / 5.0, -1.0 / 5.0, 8.0 / 315.0, -1.0 / 560.0)
COEF_FIRST = (4.0 / 5.0, -1.0 / 5.0, 4.0 / 105.0, -1.0 / 280.0)
SPEED_SCALE = 0.12
F32 = jnp.float32
BF16 = jnp.bfloat16
LEVELS = 32767.0
SMALLEST = 1e-30
MESH = pl.DeviceIdType.MESH
PLANES = 8
CHUNKS = NX // PLANES
ROWS = PLANES * NY
UNROLL = 8
DEPTH_CHIPS = 8
TURNED = tuple((8 - i) % 8 for i in range(8))


def band(extent, centre):
    second = np.zeros((extent, extent))
    first = np.zeros((extent, extent))
    for to in range(extent):
        second[to, to] = centre
        for reach in range(1, 5):
            if to + reach < extent:
                second[to, to + reach] = COEF_SECOND[reach]
                first[to, to + reach] = COEF_FIRST[reach - 1]
            if to - reach >= 0:
                second[to, to - reach] = COEF_SECOND[reach]
                first[to, to - reach] = -COEF_FIRST[reach - 1]
    return second, first


def parts_of(matrix):
    high = matrix.astype(ml_dtypes.bfloat16)
    low = (matrix - high.astype(np.float64)).astype(ml_dtypes.bfloat16)
    return high, low


def depth_matrix():
    second, first = band(NZ, 3.0 * COEF_SECOND[0])
    high, low = parts_of(np.concatenate([second.T, first.T], axis=1))
    return np.concatenate([high, high, low], axis=0)


def middle_matrix():
    second, first = band(NY, 0.0)
    eight = np.eye(PLANES)
    both = np.stack([np.kron(eight, second), np.kron(eight, first)])
    both = both.reshape(2, PLANES * 2, 8, ROWS).transpose(1, 0, 2, 3).reshape(2 * ROWS, ROWS)
    high, low = parts_of(both)
    return np.concatenate([high, high, low], axis=1)


def split_two(values):
    high = values.astype(BF16)
    low = (values - high.astype(F32)).astype(BF16)
    return high, low


def to_levels(values):
    return jnp.round(values).astype(jnp.int32).astype(jnp.int16)


def turn(block, lane_block):
    block = pltpu.roll(block, 0, 1, stride=B, stride_axis=0)
    for bit in (1, 2, 4):
        block = jnp.where((lane_block & bit) != 0, pltpu.roll(block, 8 - bit, 0), block)
    return pltpu.roll(block, 0, 1, stride=B, stride_axis=0)


def products(window_ref, at, depth_ref, middle_ref):
    inner = window_ref[pl.ds(at * PLANES + 4, PLANES)].reshape(ROWS, NZ)
    high, low = split_two(inner)
    along_depth = jnp.dot(
        jnp.concatenate([high, low, high], axis=1), depth_ref[...], preferred_element_type=F32
    )
    along_middle = jnp.dot(
        middle_ref[...], jnp.concatenate([high, low, high], axis=0), preferred_element_type=F32
    )
    return along_depth, along_middle


def each_block(window_ref, at, depth_ref, middle_ref, body):
    along_depth, along_middle = products(window_ref, at, depth_ref, middle_ref)
    base = at * PLANES
    window = [[window_ref[base + j, 8 * half : 8 * half + 8] for half in range(2)] for j in range(8)]
    for plane in range(PLANES):
        window.append([window_ref[base + plane + 8, 8 * half : 8 * half + 8] for half in range(2)])
        for half in range(2):
            row = (plane * 2 + half) * 8
            second = along_depth[row : row + 8, :NZ] + along_middle[2 * row : 2 * row + 8]
            first = None
            for reach in range(1, 5):
                ahead, behind = window[plane + 4 + reach][half], window[plane + 4 - reach][half]
                second = second + COEF_SECOND[reach] * (ahead + behind)
                term = COEF_FIRST[reach - 1] * (ahead - behind)
                first = term if first is None else first + term
            body(
                base + plane, slice(8 * half, 8 * half + 8), window[plane + 4][half],
                second, first, along_middle[2 * row + 8 : 2 * row + 16], along_depth[row : row + 8, NZ:],
            )


def place():
    shot, tile = lax.axis_index("shot"), lax.axis_index("tile")
    shots, depths = lax.axis_size("shot"), DEPTH_CHIPS
    across = lax.axis_size("tile") // depths
    return shot, lax.div(tile, depths), lax.rem(tile, depths), shots, across, depths


def shifted(index, by, size):
    return lax.rem(index + by, size)


def greet(shot, x, z, shots, across, depths):
    barrier = pltpu.get_barrier_semaphore()

    def signal(device_id):
        pl.semaphore_signal(barrier, inc=1, device_id=device_id, device_id_type=MESH)

    def to_shot(by, carry):
        signal((shifted(shot, by, shots), x * depths + z))
        return carry

    lax.fori_loop(1, shots, to_shot, 0)
    for by in range(1, across):
        signal((shot, shifted(x, by, across) * depths + z))
    for by in range(1, depths):
        signal((shot, x * depths + shifted(z, by, depths)))
    pl.semaphore_wait(barrier, shots + across + depths - 3)


def remote(src, dst, send_sem, recv_sem, device_id):
    return pltpu.make_async_remote_copy(
        src_ref=src, dst_ref=dst, send_sem=send_sem, recv_sem=recv_sem,
        device_id=device_id, device_id_type=MESH,
    )


def rows_at(start, size):
    return pl.ds(pl.multiple_of(start, size), size)


def row_levels(values):
    rows, lanes = values.shape
    field = lanes // 2
    units, coded = [], []
    for at in range(2):
        part = values[:, at * field : (at + 1) * field]
        largest = jnp.maximum(jnp.max(jnp.abs(part), axis=1, keepdims=True), SMALLEST)
        units.append(largest * (1.0 / LEVELS))
        coded.append(part * (LEVELS / largest))
    first = lax.broadcasted_iota(jnp.int32, (rows, NZ), 1) == 0
    lines = jnp.transpose(jnp.where(first, units[0], units[1]))[:8]
    return to_levels(jnp.concatenate(coded, axis=1)), lines


def from_levels(levels, units):
    field = levels.shape[1] // 2
    values = levels.astype(F32)
    return jnp.concatenate(
        [values[:, :field] * units[:, 0:1], values[:, field:] * units[:, 1:2]], axis=1
    )


def shot_kernel(
    block_ref, names_ref, source_ref, pulse_ref, cells_ref, traces_ref,
    fwd_hbm, adj_hbm, depth_hbm, middle_hbm,
    out_ref,
    depth_ref, middle_ref, load_sem,
    store_ref, pick_ref, names_all, outgoing, incoming, groups_ref,
    gain_ref, speed_ref, slope_ref, wave_ref, adj_ref, image_ref, first_ref, inject_ref, hot_ref,
    mask_ref, sums_ref,
    grads_ref, units_ref, grads_all, units_all, place_ref, spread_ref,
    whole, whole_levels, whole_lines, from_x, lines_x,
    column, column_levels, column_lines, from_z, lines_z, turned_units,
    z_send, z_recv, x_send, x_recv, name_send, name_recv, shot_send, shot_recv,
    grad_send, grad_recv, unit_send, unit_recv, gx_send, gx_recv, xu_send, xu_recv,
    gz_send, gz_recv, zu_send, zu_recv,
):
    shot, x, z, shots, across, depths = place()
    owned = block_ref.shape[0]
    me = x * depths + z
    positions = APX * APZ
    group = NZ // positions
    total = store_ref.shape[0]
    lane_block = lax.broadcasted_iota(jnp.int32, (8, NZ), 1) // B

    loads = [
        pltpu.make_async_copy(src, dst, load_sem.at[i])
        for i, (src, dst) in enumerate(
            [
                (depth_hbm, depth_ref),
                (middle_hbm, middle_ref),
                (fwd_hbm.at[0, 0], wave_ref.at[0, pl.ds(4, NX)]),
                (fwd_hbm.at[0, 1], wave_ref.at[1, pl.ds(4, NX)]),
                (adj_hbm.at[0, 0], adj_ref.at[0, pl.ds(4, NX)]),
                (adj_hbm.at[0, 1], adj_ref.at[1, pl.ds(4, NX)]),
            ]
        )
    ]
    for load in loads:
        load.start()

    greet(shot, x, z, shots, across, depths)

    store_ref[rows_at(me * owned, owned)] = block_ref[...]
    names_all[shot] = names_ref[...]

    def z_copy(by):
        return remote(
            block_ref, store_ref.at[rows_at(me * owned, owned)], z_send.at[by], z_recv.at[by],
            (shot, x * depths + shifted(z, by, depths)),
        )

    def name_copy(by):
        return remote(
            names_ref, names_all.at[shot], name_send.at[by], name_recv.at[by],
            (shifted(shot, by, shots), me),
        )

    def x_copy(along, by):
        rows = store_ref.at[rows_at((x * depths + shifted(z, depths - by, depths)) * owned, owned)]
        return remote(
            rows, rows, x_send.at[along, by], x_recv.at[along, by],
            (shot, shifted(x, along, across) * depths + z),
        )

    def start_z(by, carry):
        z_copy(by).start()
        return carry

    def start_name(by, carry):
        name_copy(by).start()
        return carry

    def pass_on(by, carry):
        z_copy(by).wait_recv()
        for along in range(1, across):
            x_copy(along, by).start()
        return carry

    lax.fori_loop(1, depths, start_z, 0)
    for along in range(1, across):
        x_copy(along, 0).start()
    lax.fori_loop(1, shots, start_name, 0)
    lax.fori_loop(1, depths, pass_on, 0)

    def wait_name(by, carry):
        name_copy(by).wait_recv()
        return carry

    lax.fori_loop(1, shots, wait_name, 0)

    lines, turned = [], []
    for at in range(8):
        if at < shots // group:
            lines.append(sum(names_all[group * at + i, 0:1] for i in range(group)))
            turned.append(sum(names_all[group * at + i, 1:2] for i in range(group)))
        else:
            lines.append(jnp.zeros((1, NZ), F32))
            turned.append(jnp.zeros((1, NZ), F32))
    groups_ref[...] = jnp.concatenate(turned, axis=0)
    columns = jnp.transpose(jnp.concatenate(lines, axis=0))
    row_ids = lax.broadcasted_iota(jnp.int32, (NZ, total), 1).astype(F32)
    for at in range(shots // group):
        pick_ref[at] = (row_ids == columns[:, at : at + 1]).astype(F32).astype(BF16)

    def wait_x(by, carry):
        for along in range(1, across):
            x_copy(along, by).wait_recv()
        return carry

    lax.fori_loop(0, depths, wait_x, 0)

    def choose(at, carry):
        chosen = jnp.dot(pick_ref[at], store_ref[...], preferred_element_type=F32).astype(BF16)
        outgoing[pl.ds(at * group, group)] = chosen.reshape(group, positions, chosen.shape[1])
        return carry

    lax.fori_loop(0, shots // group, choose, 0)

    def shot_copy(by):
        target = shifted(shot, by, shots)
        return remote(
            outgoing.at[target], incoming.at[shot], shot_send.at[by], shot_recv.at[by], (target, me)
        )

    def start_shot(by, carry):
        shot_copy(by).start()
        return carry

    lax.fori_loop(1, shots, start_shot, 0)
    incoming[shot] = outgoing[shot]

    border = jnp.zeros((4, NY, NZ), F32)
    for ref in (gain_ref, wave_ref.at[0], wave_ref.at[1], adj_ref.at[0], adj_ref.at[1]):
        ref[0:4] = border
        ref[NX + 4 : NX + 8] = border

    source = source_ref[0]
    lane_ids = lax.broadcasted_iota(jnp.int32, (NY, NZ), 1)
    row_of = lax.broadcasted_iota(jnp.int32, (NY, NZ), 0)

    def mark(plane, carry):
        cell = (plane * NY + row_of) * NZ + lane_ids
        mask_ref[plane] = (cell == source).astype(F32)
        return carry

    lax.fori_loop(0, NX, mark, 0)

    cells = cells_ref[...]
    cell_rows = lax.shift_right_logical(cells, 7)
    cell_lanes = jnp.transpose(jnp.broadcast_to((cells & 127).astype(F32), (8, NREC)))[:, 0:1]
    trace_columns = jnp.transpose(traces_ref[...])
    for at in range(8):
        row_ids = lax.broadcasted_iota(jnp.int32, (128, NREC), 0) + at * 128
        hot_ref[at * 128 : at * 128 + 128] = (row_ids == cell_rows).astype(F32).astype(BF16)
    lane_hot = lax.broadcasted_iota(jnp.int32, (NREC, NZ), 1).astype(F32) == cell_lanes
    for step in range(STEPS):
        high, low = split_two(jnp.where(lane_hot, trace_columns[:, step : step + 1], 0.0))
        both = jnp.concatenate([high, low], axis=1)
        added = jnp.dot(hot_ref[...], both, preferred_element_type=F32)
        inject_ref[step] = (added[:, :NZ] + added[:, NZ:]).reshape(NX, NY, NZ)

    store_rows = lax.broadcasted_iota(jnp.int32, (total, NZ), 0).astype(F32)
    for at in range(shots // group):
        hot = (store_rows == groups_ref[at : at + 1]).astype(F32).astype(BF16)
        for part in range(2):
            lanes = (part * (shots // group) + at) * NZ
            place_ref[:, lanes : lanes + NZ] = hot

    def unpack(by, carry):
        plane = shifted(shot, shots - by, shots)
        for block in range(APX):
            at = block * B + plane
            for field in range(2):
                for half in range(2):
                    lanes = (field * 2 + half) * NZ
                    rows_of = incoming[plane, block * 8 : block * 8 + 8, lanes : lanes + NZ].astype(F32)
                    turned = turn(rows_of, lane_block)
                    if field == 0:
                        speed_ref[at, half * 8 : half * 8 + 8] = SPEED_SCALE * turned
                    else:
                        gain_ref[at + 4, half * 8 : half * 8 + 8] = turned
        return carry

    unpack(0, 0)

    def arrived(by, carry):
        shot_copy(by).wait_recv()
        return unpack(by, carry)

    lax.fori_loop(1, shots, arrived, 0)

    for load in loads:
        load.wait()

    def run(window_ref, body):
        def chunk(at, carry):
            each_block(window_ref, at, depth_ref, middle_ref, body)
            return carry

        lax.fori_loop(0, CHUNKS, chunk, 0, unroll=UNROLL)

    def slopes(plane, rows, centre, second, *firsts):
        for axis in range(3):
            slope_ref[axis, plane, rows] = firsts[axis]

    run(gain_ref, slopes)

    def apply(plane, rows, second, firsts):
        applied = gain_ref[plane + 4, rows] * second
        for axis in range(3):
            applied = applied + slope_ref[axis, plane, rows] * firsts[axis]
        return applied

    def forward(step, now_ref, other_ref):
        pulse = pulse_ref[0, step]

        def body(plane, rows, centre, second, *firsts):
            applied = apply(plane, rows, second, firsts)
            image_ref[step, plane, rows] = applied
            for axis in range(3):
                first_ref[step, axis, plane, rows] = firsts[axis]
            newer = 2.0 * centre - other_ref[plane + 4, rows] + speed_ref[plane, rows] * applied
            other_ref[plane + 4, rows] = newer + pulse * mask_ref[plane, rows]

        run(now_ref, body)

    def forward_pair(pair, carry):
        forward(2 * pair, wave_ref.at[1], wave_ref.at[0])
        forward(2 * pair + 1, wave_ref.at[0], wave_ref.at[1])
        return carry

    lax.fori_loop(0, STEPS // 2, forward_pair, 0)

    def backward(step, now_ref, other_ref, start):
        def body(plane, rows, centre, second, *firsts):
            applied = apply(plane, rows, second, firsts)
            newer = 2.0 * centre - other_ref[plane + 4, rows] + speed_ref[plane, rows] * applied
            newer = newer + inject_ref[step, plane, rows]
            other_ref[plane + 4, rows] = newer
            part = newer * image_ref[step, plane, rows]
            if start:
                sums_ref[0, plane, rows] = part
            else:
                sums_ref[0, plane, rows] = sums_ref[0, plane, rows] + part
                part = firsts[0] * first_ref[step + 1, 0, plane, rows]
                part = part + firsts[1] * first_ref[step + 1, 1, plane, rows]
                part = part + firsts[2] * first_ref[step + 1, 2, plane, rows]
                sums_ref[1, plane, rows] = sums_ref[1, plane, rows] + part

        run(now_ref, body)

    def clear(plane, carry):
        sums_ref[1, plane] = jnp.zeros((NY, NZ), F32)
        return carry

    lax.fori_loop(0, NX, clear, 0)
    backward(STEPS - 1, adj_ref.at[1], adj_ref.at[0], True)

    def backward_pair(pair, carry):
        backward(STEPS - 2 - 2 * pair, adj_ref.at[0], adj_ref.at[1], False)
        backward(STEPS - 3 - 2 * pair, adj_ref.at[1], adj_ref.at[0], False)
        return carry

    lax.fori_loop(0, STEPS // 2 - 1, backward_pair, 0)
    backward(0, adj_ref.at[0], adj_ref.at[1], False)

    def last(plane, rows, centre, second, *firsts):
        part = sums_ref[1, plane, rows]
        for axis in range(3):
            part = part + firsts[axis] * first_ref[0, axis, plane, rows]
        sums_ref[1, plane, rows] = part * speed_ref[plane, rows]

    run(adj_ref.at[1], last)

    def code(plane):
        for block in range(APX):
            at = block * B + plane
            for field in range(2):
                values = sums_ref[field, at]
                largest = jnp.max(jnp.abs(values), axis=(0, 1), keepdims=True)
                largest = jnp.maximum(largest, SMALLEST)
                line = field * APX + block
                units_ref[plane, line : line + 1] = jnp.broadcast_to(largest * (1.0 / LEVELS), (1, NZ))
                grads_ref[plane, field, block] = to_levels(values * (LEVELS / largest))

    def grad_copy(by):
        target = shifted(shot, by, shots)
        return remote(
            grads_ref.at[target], grads_all.at[shot], grad_send.at[by], grad_recv.at[by], (target, me)
        )

    def unit_copy(by):
        target = shifted(shot, by, shots)
        return remote(
            units_ref.at[target], units_all.at[shot], unit_send.at[by], unit_recv.at[by], (target, me)
        )

    def start_grad(by, carry):
        code(shifted(shot, by, shots))
        grad_copy(by).start()
        unit_copy(by).start()
        return carry

    lax.fori_loop(1, shots, start_grad, 0)
    code(shot)
    grads_all[shot] = grads_ref[shot]
    units_all[shot] = units_ref[shot]

    def spread(by, carry):
        sender = shifted(shot, shots - by, shots)
        for pair in range(APX // 2):
            for field in range(2):
                halves = [[], []]
                for block in (2 * pair, 2 * pair + 1):
                    line = field * APX + block
                    values = grads_all[sender, field, block].astype(F32) * units_all[sender, line : line + 1]
                    for half in range(2):
                        halves[half].append(turn(values[8 * half : 8 * half + 8], lane_block))
                for half in range(2):
                    lanes = (field * 2 + half) * NZ
                    high, low = split_two(jnp.concatenate(halves[half], axis=0))
                    rows = pl.ds(pl.multiple_of(sender * positions + pair * 16, 16), 16)
                    spread_ref[0, rows, lanes : lanes + NZ] = high
                    spread_ref[1, rows, lanes : lanes + NZ] = low
        return carry

    spread(0, 0)

    def returned(by, carry):
        grad_copy(by).wait_recv()
        unit_copy(by).wait_recv()
        return spread(by, carry)

    lax.fori_loop(1, shots, returned, 0)

    block = depths * owned
    parts = spread_ref[...].reshape(2 * shots * positions, spread_ref.shape[2])
    for at in range(across):
        rows = slice(at * block, at * block + block)
        added = jnp.dot(place_ref[rows], parts, preferred_element_type=F32)
        whole[rows] = added
        coded, units = row_levels(added)
        whole_levels[rows] = coded
        whole_lines[at] = units

    def gx_copy(along):
        target = shifted(x, along, across)
        return remote(
            whole_levels.at[rows_at(target * block, block)], from_x.at[along],
            gx_send.at[along], gx_recv.at[along], (shot, target * depths + z),
        )

    def gx_lines(along):
        target = shifted(x, along, across)
        return remote(
            whole_lines.at[target], lines_x.at[along],
            xu_send.at[along], xu_recv.at[along], (shot, target * depths + z),
        )

    for along in range(1, across):
        gx_copy(along).start()
        gx_lines(along).start()
    summed = whole[rows_at(x * block, block)]
    for along in range(1, across):
        gx_copy(along).wait_recv()
        gx_lines(along).wait_recv()
        summed = summed + from_levels(from_x[along], jnp.transpose(lines_x[along]))
    column[...] = summed
    coded, units = row_levels(summed)
    column_levels[...] = coded
    column_lines[...] = units

    def gz_copy(by):
        target = shifted(z, by, depths)
        return remote(
            column_levels.at[rows_at(target * owned, owned)], from_z.at[by],
            gz_send.at[by], gz_recv.at[by], (shot, x * depths + target),
        )

    def gz_lines(by):
        target = shifted(z, by, depths)
        return remote(
            column_lines, lines_z.at[by], zu_send.at[by], zu_recv.at[by], (shot, x * depths + target)
        )

    for by in range(1, depths):
        gz_copy(by).start()
        gz_lines(by).start()
    mine = column[rows_at(z * owned, owned)]
    for by in range(1, depths):
        gz_copy(by).wait_recv()
        gz_lines(by).wait_recv()
        turned_units[by] = jnp.transpose(lines_z[by])
        mine = mine + from_levels(from_z[by], turned_units[by, rows_at(z * owned, owned)])
    out_ref[...] = mine

    def finish_shots(by, carry):
        shot_copy(by).wait_send()
        name_copy(by).wait_send()
        grad_copy(by).wait_send()
        unit_copy(by).wait_send()
        return carry

    def finish_z(by, carry):
        z_copy(by).wait_send()
        gz_copy(by).wait_send()
        gz_lines(by).wait_send()
        return carry

    def finish_x(by, carry):
        for along in range(1, across):
            x_copy(along, by).wait_send()
        return carry

    lax.fori_loop(1, shots, finish_shots, 0)
    lax.fori_loop(1, depths, finish_z, 0)
    lax.fori_loop(0, depths, finish_x, 0)
    for along in range(1, across):
        gx_copy(along).wait_send()
        gx_lines(along).wait_send()


def shot_gradients(block, names, source, pulses, cells, traces, fwd, adj, shots, tiles):
    vmem = pl.BlockSpec(memory_space=pltpu.VMEM)
    smem = pl.BlockSpec(memory_space=pltpu.SMEM)
    hbm = pl.BlockSpec(memory_space=pl.ANY)
    owned, lanes = block.shape
    depths = DEPTH_CHIPS
    across = tiles // depths
    total = tiles * owned
    positions = APX * APZ
    groups = shots * positions // NZ
    rows = depths * owned
    volume = (NX, NY, NZ)
    padded = (NX + 8, NY, NZ)
    int16 = jnp.int16
    dma = pltpu.SemaphoreType.DMA
    depth, middle = depth_matrix(), middle_matrix()
    return pl.pallas_call(
        shot_kernel,
        out_shape=jax.ShapeDtypeStruct((owned, lanes), F32),
        in_specs=[vmem, vmem, smem, smem, vmem, vmem, hbm, hbm, hbm, hbm],
        out_specs=vmem,
        scratch_shapes=[
            pltpu.VMEM(depth.shape, BF16),
            pltpu.VMEM(middle.shape, BF16),
            dma((6,)),
            pltpu.VMEM((total, lanes), BF16),
            pltpu.VMEM((groups, NZ, total), BF16),
            pltpu.VMEM((shots, 8, NZ), F32),
            pltpu.VMEM((shots, positions, lanes), BF16),
            pltpu.VMEM((shots, positions, lanes), BF16),
            pltpu.VMEM((8, NZ), F32),
            pltpu.VMEM(padded, F32),
            pltpu.VMEM(volume, F32),
            pltpu.VMEM((3,) + volume, F32),
            pltpu.VMEM((2,) + padded, F32),
            pltpu.VMEM((2,) + padded, F32),
            pltpu.VMEM((STEPS,) + volume, F32),
            pltpu.VMEM((STEPS, 3) + volume, F32),
            pltpu.VMEM((STEPS,) + volume, F32),
            pltpu.VMEM((NX * NY, NREC), BF16),
            pltpu.VMEM(volume, F32),
            pltpu.VMEM((2,) + volume, F32),
            pltpu.VMEM((B, 2, APX, NY, NZ), int16),
            pltpu.VMEM((B, 8, NZ), F32),
            pltpu.VMEM((shots, 2, APX, NY, NZ), int16),
            pltpu.VMEM((shots, 8, NZ), F32),
            pltpu.VMEM((total, 2 * groups * NZ), BF16),
            pltpu.VMEM((2, shots * positions, lanes), BF16),
            pltpu.VMEM((total, lanes), F32),
            pltpu.VMEM((total, lanes), int16),
            pltpu.VMEM((across, 8, rows), F32),
            pltpu.VMEM((across, rows, lanes), int16),
            pltpu.VMEM((across, 8, rows), F32),
            pltpu.VMEM((rows, lanes), F32),
            pltpu.VMEM((rows, lanes), int16),
            pltpu.VMEM((8, rows), F32),
            pltpu.VMEM((depths, owned, lanes), int16),
            pltpu.VMEM((depths, 8, rows), F32),
            pltpu.VMEM((depths, rows, 8), F32),
            dma((depths,)), dma((depths,)),
            dma((across, depths)), dma((across, depths)),
            dma((shots,)), dma((shots,)), dma((shots,)), dma((shots,)),
            dma((shots,)), dma((shots,)), dma((shots,)), dma((shots,)),
            dma((across,)), dma((across,)), dma((across,)), dma((across,)),
            dma((depths,)), dma((depths,)), dma((depths,)), dma((depths,)),
        ],
        compiler_params=pltpu.CompilerParams(
            collective_id=0, has_side_effects=True, vmem_limit_bytes=56 * 1024 * 1024
        ),
        cost_estimate=pl.CostEstimate(flops=2 * 10**9, bytes_accessed=5 * 2**20, transcendentals=0),
        name="shot_gradients",
    )(block, names, source, pulses, cells, traces, fwd, adj, jnp.asarray(depth), jnp.asarray(middle))


def per_device(
    tile_store, apertures, model, fwd_states, adj_states, source_cell, wavelet, receiver_cells, residuals
):
    shot = lax.axis_index("shot")
    shots, tiles = lax.axis_size("shot"), lax.axis_size("tile")
    owned = model.shape[0]
    positions = APX * APZ
    cells = model.shape[2] // shots

    rows = tile_store[apertures[0]].astype(F32)
    turned = rows.reshape(APX, APZ)
    turned = jnp.concatenate([turned[:, :1], turned[:, :0:-1]], axis=1).reshape(positions)
    group = NZ // positions
    mine = jnp.repeat(jnp.arange(group) == lax.rem(shot, group), positions)
    lines = [jnp.where(mine, jnp.tile(line, group), 0.0) for line in (rows, turned)]
    names = jnp.concatenate([jnp.stack(lines), jnp.zeros((6, NZ), F32)])

    block = lax.dynamic_slice_in_dim(model, shot * cells, cells, axis=2)
    block = block.reshape(owned, 4, 8, B)
    block = jnp.concatenate([block[:, :, :1], block[:, :, :0:-1]], axis=2).reshape(owned, 2 * cells)

    sums = shot_gradients(
        block, names, source_cell, wavelet, receiver_cells, residuals[0], fwd_states, adj_states,
        shots, tiles,
    )
    return sums.reshape(owned, 2, cells)


def solution(mesh):
    return jax.shard_map(
        per_device,
        mesh=mesh,
        in_specs=(
            P(),
            P(("shot", "tile"), None),
            P("tile", None, None),
            P(("shot", "tile"), None, None, None, None),
            P(("shot", "tile"), None, None, None, None),
            P(("shot", "tile")),
            P(("shot", "tile"), None),
            P(("shot", "tile"), None),
            P(("shot", "tile"), None, None),
        ),
        out_specs=P("tile", None, "shot"),
        check_vma=False,
    )
```

```python
import jax
import jax.numpy as jnp
import ml_dtypes
import numpy as np
from jax import lax
from jax.experimental import pallas as pl
from jax.experimental.pallas import tpu as pltpu
from jax.sharding import PartitionSpec as P

B = 16
APX = 4
APZ = 8
NX, NY, NZ = 64, 16, 128
STEPS = 8
NREC = 256
COEF_SECOND = (-205.0 / 72.0, 8.0 / 5.0, -1.0 / 5.0, 8.0 / 315.0, -1.0 / 560.0)
COEF_FIRST = (4.0 / 5.0, -1.0 / 5.0, 4.0 / 105.0, -1.0 / 280.0)
SPEED_SCALE = 0.12
F32 = jnp.float32
BF16 = jnp.bfloat16
LEVELS = 32767.0
SMALLEST = 1e-30
MESH = pl.DeviceIdType.MESH
PLANES = 8
CHUNKS = NX // PLANES
ROWS = PLANES * NY
UNROLL = 8
DEPTH_CHIPS = 8
TURNED = tuple((8 - i) % 8 for i in range(8))


def band(extent, centre):
    second = np.zeros((extent, extent))
    first = np.zeros((extent, extent))
    for to in range(extent):
        second[to, to] = centre
        for reach in range(1, 5):
            if to + reach < extent:
                second[to, to + reach] = COEF_SECOND[reach]
                first[to, to + reach] = COEF_FIRST[reach - 1]
            if to - reach >= 0:
                second[to, to - reach] = COEF_SECOND[reach]
                first[to, to - reach] = -COEF_FIRST[reach - 1]
    return second, first


def parts_of(matrix):
    high = matrix.astype(ml_dtypes.bfloat16)
    low = (matrix - high.astype(np.float64)).astype(ml_dtypes.bfloat16)
    return high, low


def depth_matrix():
    second, first = band(NZ, 3.0 * COEF_SECOND[0])
    high, low = parts_of(np.concatenate([second.T, first.T], axis=1))
    return np.concatenate([high, high, low], axis=0)


def middle_matrix():
    second, first = band(NY, 0.0)
    eight = np.eye(PLANES)
    both = np.stack([np.kron(eight, second), np.kron(eight, first)])
    both = both.reshape(2, PLANES * 2, 8, ROWS).transpose(1, 0, 2, 3).reshape(2 * ROWS, ROWS)
    high, low = parts_of(both)
    return np.concatenate([high, high, low], axis=1)


def split_two(values):
    high = values.astype(BF16)
    low = (values - high.astype(F32)).astype(BF16)
    return high, low


def to_levels(values):
    return jnp.round(values).astype(jnp.int32).astype(jnp.int16)


def turn(block, lane_block):
    block = pltpu.roll(block, 0, 1, stride=B, stride_axis=0)
    for bit in (1, 2, 4):
        block = jnp.where((lane_block & bit) != 0, pltpu.roll(block, 8 - bit, 0), block)
    return pltpu.roll(block, 0, 1, stride=B, stride_axis=0)


def products(window_ref, at, depth_ref, middle_ref):
    inner = window_ref[pl.ds(at * PLANES + 4, PLANES)].reshape(ROWS, NZ)
    high, low = split_two(inner)
    along_depth = jnp.dot(
        jnp.concatenate([high, low, high], axis=1), depth_ref[...], preferred_element_type=F32
    )
    along_middle = jnp.dot(
        middle_ref[...], jnp.concatenate([high, low, high], axis=0), preferred_element_type=F32
    )
    return along_depth, along_middle


def each_block(window_ref, at, depth_ref, middle_ref, body):
    along_depth, along_middle = products(window_ref, at, depth_ref, middle_ref)
    base = at * PLANES
    window = [[window_ref[base + j, 8 * half : 8 * half + 8] for half in range(2)] for j in range(8)]
    for plane in range(PLANES):
        window.append([window_ref[base + plane + 8, 8 * half : 8 * half + 8] for half in range(2)])
        for half in range(2):
            row = (plane * 2 + half) * 8
            second = along_depth[row : row + 8, :NZ] + along_middle[2 * row : 2 * row + 8]
            first = None
            for reach in range(1, 5):
                ahead, behind = window[plane + 4 + reach][half], window[plane + 4 - reach][half]
                second = second + COEF_SECOND[reach] * (ahead + behind)
                term = COEF_FIRST[reach - 1] * (ahead - behind)
                first = term if first is None else first + term
            body(
                base + plane, slice(8 * half, 8 * half + 8), window[plane + 4][half],
                second, first, along_middle[2 * row + 8 : 2 * row + 16], along_depth[row : row + 8, NZ:],
            )


def place():
    shot, tile = lax.axis_index("shot"), lax.axis_index("tile")
    return lax.div(shot, 2), lax.rem(shot, 2), lax.div(tile, DEPTH_CHIPS), lax.rem(tile, DEPTH_CHIPS)


def shifted(index, by, size):
    return lax.rem(index + by, size)


def chunk_of(route, index, y):
    if route == 0:
        return index
    return lax.rem(3 * y + lax.div(index, 2), DEPTH_CHIPS) * 2 + lax.rem(index, 2)


def greet(y, core, x, z, shots, across, depths):
    barrier = pltpu.get_barrier_semaphore()
    shot, turned_shot = y * 2 + core, z * 2 + core

    def signal(device_id):
        pl.semaphore_signal(barrier, inc=1, device_id=device_id, device_id_type=MESH)

    for by in range(1, depths):
        signal((shot, x * depths + shifted(z, by, depths)))
    for by in range(1, across):
        signal((shot, shifted(x, by, across) * depths + z))

    def to_columns(by, carry):
        signal((shifted(shot, by, shots), x * depths + z))
        other = shifted(turned_shot, by, shots)
        signal((y * 2 + lax.rem(other, 2), x * depths + lax.div(other, 2)))
        return carry

    lax.fori_loop(1, shots, to_columns, 0)
    home = lax.rem(3 * y + z, depths)

    def to_last(from_y, carry):
        @pl.when(jnp.logical_or(from_y != y, home != y))
        def _():
            signal((from_y * 2 + core, x * depths + lax.rem(y + 3 * depths - 3 * from_y, depths)))

        return carry

    lax.fori_loop(0, depths, to_last, 0)
    here = jnp.where(home == y, 1, 0)
    return barrier, 2 * (shots - 1) + across - 1 + depths - 1 + depths - here


def remote(src, dst, send_sem, recv_sem, device_id):
    return pltpu.make_async_remote_copy(
        src_ref=src, dst_ref=dst, send_sem=send_sem, recv_sem=recv_sem,
        device_id=device_id, device_id_type=MESH,
    )


def rows_at(start, size):
    return pl.ds(pl.multiple_of(start, size), size)


def row_levels(values):
    rows, lanes = values.shape
    lane = lax.broadcasted_iota(jnp.int32, (rows, NZ), 1)
    coded, units = [], jnp.zeros((rows, NZ), F32)
    for at in range(lanes // NZ):
        part = values[:, at * NZ : (at + 1) * NZ]
        largest = jnp.maximum(jnp.max(jnp.abs(part), axis=1, keepdims=True), SMALLEST)
        units = jnp.where(lane == at, largest * (1.0 / LEVELS), units)
        coded.append(part * (LEVELS / largest))
    return to_levels(jnp.concatenate(coded, axis=1)), jnp.transpose(units)[:8]


def from_levels(levels, units):
    values = levels.astype(F32)
    return jnp.concatenate(
        [values[:, at * NZ : (at + 1) * NZ] * units[:, at : at + 1] for at in range(values.shape[1] // NZ)],
        axis=1,
    )


def shot_kernel(
    tile_store_ref, aperture_ref, model_ref, source_ref, pulse_ref, cells_ref, traces_ref,
    fwd_hbm, adj_hbm, depth_hbm, middle_hbm,
    out_ref,
    depth_ref, middle_ref, depth_f32, middle_f32, load_sem,
    blocks_ref, names_ref, store_ref, pick_ref, names_all, outgoing, incoming,
    gain_ref, speed_ref, slope_ref, wave_ref, adj_ref, image_ref, first_ref, inject_ref, hot_ref,
    mask_ref, sums_ref,
    grads_ref, units_ref, grads_all, units_all, place_ref, spread_ref,
    whole_levels, whole_lines, from_x, lines_x, column, from_z,
    z_send, z_recv, x_send, x_recv, name_send, name_recv, shot_send, shot_recv,
    grad_send, grad_recv, unit_send, unit_recv, gx_send, gx_recv, xu_send, xu_recv,
    gz_send, gz_recv,
):
    y, core, x, z = place()
    shots, across, depths = names_all.shape[1], from_x.shape[1], DEPTH_CHIPS
    owned = model_ref.shape[0]
    me = x * depths + z
    positions = APX * APZ
    group = NZ // positions
    total = store_ref.shape[0] * owned
    cells_of = model_ref.shape[1] // 2
    lane_block = lax.broadcasted_iota(jnp.int32, (8, NZ), 1) // B

    mine = (y * 2 + core, z * 2 + core)

    def on_route(route, index):
        if route == 0:
            return (index, me)
        return (y * 2 + lax.rem(index, 2), x * depths + lax.div(index, 2))

    loads = [
        pltpu.make_async_copy(src, dst, load_sem.at[i])
        for i, (src, dst) in enumerate(
            [
                (depth_hbm, depth_f32),
                (middle_hbm, middle_f32),
                (fwd_hbm.at[0, 0], wave_ref.at[0, pl.ds(4, NX)]),
                (fwd_hbm.at[0, 1], wave_ref.at[1, pl.ds(4, NX)]),
                (adj_hbm.at[0, 0], adj_ref.at[0, pl.ds(4, NX)]),
                (adj_hbm.at[0, 1], adj_ref.at[1, pl.ds(4, NX)]),
            ]
        )
    ]
    barrier, greeted = greet(y, core, x, z, shots, across, depths)
    for load in loads:
        load.start()

    from_lane = lax.broadcasted_iota(jnp.int32, (NZ, NZ), 0)
    to_lane = lax.broadcasted_iota(jnp.int32, (NZ, NZ), 1)
    mirror = (from_lane % B == to_lane % B) & (from_lane // B == (8 - to_lane // B) % 8)
    mirror = mirror.astype(F32).astype(BF16)

    def cut(chunk, route):
        parts = []
        for field in range(2):
            start = pl.multiple_of(field * cells_of + chunk * 2 * NZ + route * NZ, NZ)
            parts.append(model_ref[:, pl.ds(start, NZ)])
        return jnp.concatenate(parts, axis=0)

    cuts = [cut(mine[0], 0)] + [
        cut(chunk_of(1, to * 2 + core, y), 1) for to in range(depths)
    ]
    mirrored = jnp.dot(jnp.concatenate(cuts, axis=0), mirror, preferred_element_type=F32).astype(BF16)
    for to in range(depths):
        for route in range(2):
            for field in range(2):
                row = ((route * (to + 1)) * 2 + field) * owned
                blocks_ref[to, route, :, field * NZ : field * NZ + NZ] = mirrored[row : row + owned]

    wanted = jnp.concatenate([aperture_ref[...]] * group, axis=1)
    tile_ids = lax.broadcasted_iota(jnp.int32, (total, NZ), 0)
    chosen = (tile_ids == wanted).astype(F32).astype(BF16)
    digits = jnp.broadcast_to(tile_store_ref[...], (8, total))
    digit_row = lax.broadcasted_iota(jnp.int32, (8, total), 0)
    digits = jnp.where(digit_row == 0, lax.shift_right_logical(digits, 4), digits & 15)
    found = jnp.dot(digits.astype(F32).astype(BF16), chosen, preferred_element_type=F32)
    turn_lanes = (from_lane // 8 == to_lane // 8) & (from_lane % 8 == (8 - to_lane % 8) % 8)
    found_turned = jnp.dot(
        found.astype(BF16), turn_lanes.astype(F32).astype(BF16), preferred_element_type=F32
    )
    lane_group = lax.broadcasted_iota(jnp.int32, (1, NZ), 1) // positions
    for route in range(2):
        member = lane_group == lax.rem(mine[route], group)
        for kind, digits_of in enumerate((found, found_turned)):
            line = 16.0 * digits_of[0:1] + digits_of[1:2]
            names_ref[2 * route + kind : 2 * route + kind + 1] = jnp.where(member, line, 0.0)

    pl.semaphore_wait(barrier, greeted)

    store_ref[me] = blocks_ref[z]
    for route in range(2):
        names_all[route, mine[route]] = names_ref[...]

    def z_copy(by):
        target = shifted(z, by, depths)
        return remote(
            blocks_ref.at[target], store_ref.at[me],
            z_send.at[by], z_recv.at[by], (mine[0], x * depths + target),
        )

    def name_copy(route, by):
        return remote(
            names_ref, names_all.at[route, mine[route]],
            name_send.at[route, by], name_recv.at[route, by],
            on_route(route, shifted(mine[route], by, shots)),
        )

    def x_copy(route, along):
        part = store_ref.at[pl.ds(x * depths, depths), route]
        return remote(
            part, part, x_send.at[route, along], x_recv.at[route, along],
            (mine[0], shifted(x, along, across) * depths + z),
        )

    def start_z(by, carry):
        z_copy(by).start()
        return carry

    def start_name(by, carry):
        for route in range(2):
            name_copy(route, by).start()
        return carry

    def wait_z(by, carry):
        z_copy(by).wait_recv()
        return carry

    lax.fori_loop(1, depths, start_z, 0)
    lax.fori_loop(1, shots, start_name, 0)
    lax.fori_loop(1, depths, wait_z, 0)
    for route in range(2):
        for along in (2, 1, 3):
            x_copy(route, along).start()

    def wait_name(by, carry):
        for route in range(2):
            name_copy(route, by).wait_recv()
        return carry

    lax.fori_loop(1, shots, wait_name, 0)

    groups = shots // group
    lines = [
        sum(names_all[route, group * at + i, 2 * route : 2 * route + 1] for i in range(group))
        for route in range(2)
        for at in range(groups)
    ]
    columns = jnp.transpose(jnp.concatenate(lines, axis=0))
    row_ids = lax.broadcasted_iota(jnp.int32, (NZ, total), 1).astype(F32)
    for route in range(2):
        for at in range(groups):
            column_at = route * groups + at
            hot = (row_ids == columns[:, column_at : column_at + 1]).astype(F32).astype(BF16)
            pick_ref[route, at * NZ : at * NZ + NZ] = hot

    def shot_copy(route, by):
        target = shifted(mine[route], by, shots)
        return remote(
            outgoing.at[route, target], incoming.at[route, mine[route]],
            shot_send.at[route, by], shot_recv.at[route, by], on_route(route, target),
        )

    for route in range(2):
        for along in (1, 3, 2):
            x_copy(route, along).wait_recv()
        held = store_ref[:, route].reshape(total, 2 * NZ)
        picked = jnp.dot(pick_ref[route], held, preferred_element_type=F32)
        outgoing[route] = picked.astype(BF16).reshape(shots, positions, 2 * NZ)

        def start_shot(by, carry):
            shot_copy(route, by).start()
            return carry

        lax.fori_loop(1, shots, start_shot, 0)
    for route in range(2):
        incoming[route, mine[route]] = outgoing[route, mine[route]]

    for load in loads:
        load.wait()
    depth_ref[...] = depth_f32[...].astype(BF16)
    middle_ref[...] = middle_f32[...].astype(BF16)
    border = jnp.zeros((4, NY, NZ), F32)
    for ref in (gain_ref, wave_ref.at[0], wave_ref.at[1], adj_ref.at[0], adj_ref.at[1]):
        ref[0:4] = border
        ref[NX + 4 : NX + 8] = border

    source = source_ref[0]
    lane_ids = lax.broadcasted_iota(jnp.int32, (NY, NZ), 1)
    row_of = lax.broadcasted_iota(jnp.int32, (NY, NZ), 0)

    def mark(plane, carry):
        cell = (plane * NY + row_of) * NZ + lane_ids
        mask_ref[plane] = (cell == source).astype(F32)
        sums_ref[1, plane] = jnp.zeros((NY, NZ), F32)
        return carry

    lax.fori_loop(0, NX, mark, 0)

    cells = cells_ref[...]
    cell_rows = lax.shift_right_logical(cells, 7)
    cell_lanes = jnp.transpose(jnp.broadcast_to((cells & 127).astype(F32), (8, NREC)))[:, 0:1]
    trace_columns = jnp.transpose(traces_ref[...])
    for at in range(8):
        row_ids = lax.broadcasted_iota(jnp.int32, (128, NREC), 0) + at * 128
        hot_ref[at * 128 : at * 128 + 128] = (row_ids == cell_rows).astype(F32).astype(BF16)
    lane_hot = lax.broadcasted_iota(jnp.int32, (NREC, NZ), 1).astype(F32) == cell_lanes
    for step in range(STEPS):
        high, low = split_two(jnp.where(lane_hot, trace_columns[:, step : step + 1], 0.0))
        both = jnp.concatenate([high, low], axis=1)
        added = jnp.dot(hot_ref[...], both, preferred_element_type=F32)
        inject_ref[step] = (added[:, :NZ] + added[:, NZ:]).reshape(NX, NY, NZ)

    store_rows = lax.broadcasted_iota(jnp.int32, (total, NZ), 0).astype(F32)
    for route in range(2):
        for at in range(groups):
            line = sum(names_all[route, group * at + i, 2 * route + 1 : 2 * route + 2] for i in range(group))
            hot = (store_rows == line).astype(F32).astype(BF16)
            for part in range(2):
                lanes = (part * groups + at) * NZ
                place_ref[route, :, lanes : lanes + NZ] = hot

    def unpack(route, by):
        sender = shifted(mine[route], shots - by, shots)
        plane = chunk_of(route, sender, y)
        for block in range(APX):
            at = block * B + plane
            for field in range(2):
                part = incoming[route, sender, block * 8 : block * 8 + 8, field * NZ : field * NZ + NZ]
                turned = turn(part.astype(F32), lane_block)
                if field == 0:
                    speed_ref[at, 8 * route : 8 * route + 8] = SPEED_SCALE * turned
                else:
                    gain_ref[at + 4, 8 * route : 8 * route + 8] = turned

    def arrived(by, carry):
        for route in range(2):
            shot_copy(route, by).wait_recv()
            unpack(route, by)
        return carry

    for route in range(2):
        unpack(route, 0)
    lax.fori_loop(1, shots, arrived, 0)

    def run(window_ref, body):
        def chunk(at, carry):
            each_block(window_ref, at, depth_ref, middle_ref, body)
            return carry

        lax.fori_loop(0, CHUNKS, chunk, 0, unroll=UNROLL)

    def slopes(plane, rows, centre, second, *firsts):
        for axis in range(3):
            slope_ref[axis, plane, rows] = firsts[axis]

    run(gain_ref, slopes)

    def apply(plane, rows, second, firsts):
        applied = gain_ref[plane + 4, rows] * second
        for axis in range(3):
            applied = applied + slope_ref[axis, plane, rows] * firsts[axis]
        return applied

    def forward(step, now_ref, other_ref):
        pulse = pulse_ref[0, step]

        def body(plane, rows, centre, second, *firsts):
            applied = apply(plane, rows, second, firsts)
            image_ref[step, plane, rows] = applied
            for axis in range(3):
                first_ref[step, axis, plane, rows] = firsts[axis]
            newer = 2.0 * centre - other_ref[plane + 4, rows] + speed_ref[plane, rows] * applied
            other_ref[plane + 4, rows] = newer + pulse * mask_ref[plane, rows]

        run(now_ref, body)

    def forward_pair(pair, carry):
        forward(2 * pair, wave_ref.at[1], wave_ref.at[0])
        forward(2 * pair + 1, wave_ref.at[0], wave_ref.at[1])
        return carry

    lax.fori_loop(0, STEPS // 2, forward_pair, 0)

    def backward(step, now_ref, other_ref, start):
        def body(plane, rows, centre, second, *firsts):
            applied = apply(plane, rows, second, firsts)
            newer = 2.0 * centre - other_ref[plane + 4, rows] + speed_ref[plane, rows] * applied
            newer = newer + inject_ref[step, plane, rows]
            other_ref[plane + 4, rows] = newer
            part = newer * image_ref[step, plane, rows]
            if start:
                sums_ref[0, plane, rows] = part
            else:
                sums_ref[0, plane, rows] = sums_ref[0, plane, rows] + part
                part = firsts[0] * first_ref[step + 1, 0, plane, rows]
                part = part + firsts[1] * first_ref[step + 1, 1, plane, rows]
                part = part + firsts[2] * first_ref[step + 1, 2, plane, rows]
                sums_ref[1, plane, rows] = sums_ref[1, plane, rows] + part

        run(now_ref, body)

    backward(STEPS - 1, adj_ref.at[1], adj_ref.at[0], True)

    def backward_pair(pair, carry):
        backward(STEPS - 2 - 2 * pair, adj_ref.at[0], adj_ref.at[1], False)
        backward(STEPS - 3 - 2 * pair, adj_ref.at[1], adj_ref.at[0], False)
        return carry

    lax.fori_loop(0, STEPS // 2 - 1, backward_pair, 0)
    backward(0, adj_ref.at[0], adj_ref.at[1], False)

    def last(plane, rows, centre, second, *firsts):
        part = sums_ref[1, plane, rows]
        for axis in range(3):
            part = part + firsts[axis] * first_ref[0, axis, plane, rows]
        sums_ref[1, plane, rows] = part * speed_ref[plane, rows]

    run(adj_ref.at[1], last)

    def code(route, index):
        plane = chunk_of(route, index, y)
        for field in range(2):
            values = [
                sums_ref[field, block * B + plane, 8 * route : 8 * route + 8] for block in range(APX)
            ]
            largest = jnp.abs(values[0])
            for value in values[1:]:
                largest = jnp.maximum(largest, jnp.abs(value))
            largest = jnp.maximum(jnp.max(largest, axis=(0, 1), keepdims=True), SMALLEST)
            units_ref[route, index, field : field + 1] = jnp.broadcast_to(largest * (1.0 / LEVELS), (1, NZ))
            levels = LEVELS / largest
            for pair in range(APX // 2):
                both = jnp.concatenate(values[2 * pair : 2 * pair + 2], axis=0)
                grads_ref[route, index, field, pair] = to_levels(both * levels)

    def grad_copy(route, by):
        target = shifted(mine[route], by, shots)
        return remote(
            grads_ref.at[route, target], grads_all.at[route, mine[route]],
            grad_send.at[route, by], grad_recv.at[route, by], on_route(route, target),
        )

    def unit_copy(route, by):
        target = shifted(mine[route], by, shots)
        return remote(
            units_ref.at[route, target], units_all.at[route, mine[route]],
            unit_send.at[route, by], unit_recv.at[route, by], on_route(route, target),
        )

    def start_grad(by, carry):
        for route in range(2):
            code(route, shifted(mine[route], by, shots))
            grad_copy(route, by).start()
            unit_copy(route, by).start()
        return carry

    lax.fori_loop(1, shots, start_grad, 0)
    for route in range(2):
        code(route, mine[route])
        grads_all[route, mine[route]] = grads_ref[route, mine[route]]
        units_all[route, mine[route]] = units_ref[route, mine[route]]

    def spread(route, by):
        sender = shifted(mine[route], shots - by, shots)
        for field in range(2):
            unit = units_all[route, sender, field : field + 1]
            for pair in range(APX // 2):
                values = grads_all[route, sender, field, pair].astype(F32) * unit
                turned = [turn(values[8 * i : 8 * i + 8], lane_block) for i in range(2)]
                high, low = split_two(jnp.concatenate(turned, axis=0))
                rows = pl.ds(pl.multiple_of(sender * positions + pair * 16, 16), 16)
                spread_ref[route, 0, rows, field * NZ : field * NZ + NZ] = high
                spread_ref[route, 1, rows, field * NZ : field * NZ + NZ] = low

    def returned(by, carry):
        for route in range(2):
            grad_copy(route, by).wait_recv()
            unit_copy(route, by).wait_recv()
            spread(route, by)
        return carry

    for route in range(2):
        spread(route, 0)
    lax.fori_loop(1, shots, returned, 0)

    block = depths * owned
    parts = [spread_ref[route].reshape(2 * shots * positions, 2 * NZ) for route in range(2)]

    def gx_copy(route, along):
        target = shifted(x, along, across)
        return remote(
            whole_levels.at[route, rows_at(target * block, block)], from_x.at[route, along],
            gx_send.at[route, along], gx_recv.at[route, along], (mine[0], target * depths + z),
        )

    def gx_lines(route, along):
        target = shifted(x, along, across)
        return remote(
            whole_lines.at[route, target], lines_x.at[route, along],
            xu_send.at[route, along], xu_recv.at[route, along], (mine[0], target * depths + z),
        )

    def merge(route, along):
        target = shifted(x, along, across)
        rows = rows_at(target * block, block)
        added = jnp.dot(place_ref[route, rows], parts[route], preferred_element_type=F32)
        if along == 0:
            column[route] = added
            return
        coded, units = row_levels(added)
        whole_levels[route, rows] = coded
        whole_lines[route, target] = units
        gx_copy(route, along).start()
        gx_lines(route, along).start()

    for route in range(2):
        for along in (2, 1, 3):
            merge(route, along)
    for route in range(2):
        merge(route, 0)

    def sum_x(route):
        summed = column[route]
        for along in (1, 3, 2):
            gx_copy(route, along).wait_recv()
            gx_lines(route, along).wait_recv()
            summed = summed + from_levels(from_x[route, along], jnp.transpose(lines_x[route, along]))
        column[route] = summed

    home = lax.rem(3 * y + z, depths)

    def gz_copy(by):
        target = shifted(z, by, depths)
        return remote(
            column.at[0, rows_at(target * owned, owned)], from_z.at[0, by],
            gz_send.at[0, by], gz_recv.at[0, by], (mine[0], x * depths + target),
        )

    def gy_copy(by):
        target = shifted(z, by, depths)
        return remote(
            column.at[1, rows_at(target * owned, owned)], from_z.at[1, y],
            gz_send.at[1, by], gz_recv.at[1, y], (home * 2 + core, x * depths + target),
        )

    def gy_arrival(from_y):
        return remote(
            column.at[1, rows_at(z * owned, owned)], from_z.at[1, from_y],
            gz_send.at[1, 0], gz_recv.at[1, from_y], (home * 2 + core, x * depths + shifted(z, 1, depths)),
        )

    def start_gz(by, carry):
        gz_copy(by).start()
        return carry

    def start_gy(by, carry):
        gy_copy(by).start()
        return carry

    sum_x(0)
    lax.fori_loop(1, depths, start_gz, 0)
    sum_x(1)
    lax.fori_loop(1, depths, start_gy, 0)

    @pl.when(home != y)
    def _():
        gy_copy(0).start()

    from_z[0, 0] = column[0, rows_at(z * owned, owned)]

    @pl.when(home == y)
    def _():
        from_z[1, y] = column[1, rows_at(z * owned, owned)]

    def end_z(by, carry):
        gz_copy(by).wait_recv()
        return carry

    def end_y(from_y, carry):
        @pl.when(jnp.logical_or(from_y != y, home != y))
        def _():
            gy_arrival(from_y).wait_recv()

        return carry

    lax.fori_loop(1, depths, end_z, 0)
    lax.fori_loop(0, depths, end_y, 0)
    for route in range(2):
        ended = from_z[route, 0]
        for by in range(1, depths):
            ended = ended + from_z[route, by]
        for field in range(2):
            lanes = (2 * field + route) * NZ
            out_ref[:, lanes : lanes + NZ] = ended[:, field * NZ : field * NZ + NZ]

    def finish_shots(by, carry):
        for route in range(2):
            shot_copy(route, by).wait_send()
            name_copy(route, by).wait_send()
            grad_copy(route, by).wait_send()
            unit_copy(route, by).wait_send()
        return carry

    def finish_z(by, carry):
        z_copy(by).wait_send()
        gz_copy(by).wait_send()
        gy_copy(by).wait_send()
        return carry

    lax.fori_loop(1, shots, finish_shots, 0)
    lax.fori_loop(1, depths, finish_z, 0)
    for route in range(2):
        for along in range(1, across):
            x_copy(route, along).wait_send()
            gx_copy(route, along).wait_send()
            gx_lines(route, along).wait_send()

    @pl.when(home != y)
    def _():
        gy_copy(0).wait_send()


def shot_gradients(tile_store, aperture, model, source, pulses, cells, traces, fwd, adj, shots, tiles):
    vmem = pl.BlockSpec(memory_space=pltpu.VMEM)
    smem = pl.BlockSpec(memory_space=pltpu.SMEM)
    hbm = pl.BlockSpec(memory_space=pltpu.HBM)
    owned = model.shape[0]
    lanes = model.shape[1] // shots
    depths = DEPTH_CHIPS
    across = tiles // depths
    total = tiles * owned
    positions = APX * APZ
    groups = shots * positions // NZ
    rows = depths * owned
    volume = (NX, NY, NZ)
    padded = (NX + 8, NY, NZ)
    int16 = jnp.int16
    dma = pltpu.SemaphoreType.DMA
    depth, middle = depth_matrix(), middle_matrix()
    return pl.pallas_call(
        shot_kernel,
        out_shape=jax.ShapeDtypeStruct((owned, lanes), F32),
        in_specs=[vmem, vmem, vmem, smem, smem, vmem, vmem, hbm, hbm, hbm, hbm],
        out_specs=vmem,
        scratch_shapes=[
            pltpu.VMEM(depth.shape, BF16),
            pltpu.VMEM(middle.shape, BF16),
            pltpu.VMEM(depth.shape, F32),
            pltpu.VMEM(middle.shape, F32),
            dma((6,)),
            pltpu.VMEM((depths, 2, owned, 2 * NZ), BF16),
            pltpu.VMEM((8, NZ), F32),
            pltpu.VMEM((tiles, 2, owned, 2 * NZ), BF16),
            pltpu.VMEM((2, shots * positions, total), BF16),
            pltpu.VMEM((2, shots, 8, NZ), F32),
            pltpu.VMEM((2, shots, positions, 2 * NZ), BF16),
            pltpu.VMEM((2, shots, positions, 2 * NZ), BF16),
            pltpu.VMEM(padded, F32),
            pltpu.VMEM(volume, F32),
            pltpu.VMEM((3,) + volume, F32),
            pltpu.VMEM((2,) + padded, F32),
            pltpu.VMEM((2,) + padded, F32),
            pltpu.VMEM((STEPS,) + volume, F32),
            pltpu.VMEM((STEPS, 3) + volume, F32),
            pltpu.VMEM((STEPS,) + volume, F32),
            pltpu.VMEM((NX * NY, NREC), BF16),
            pltpu.VMEM(volume, F32),
            pltpu.VMEM((2,) + volume, F32),
            pltpu.VMEM((2, B, 2, APX // 2, 16, NZ), int16),
            pltpu.VMEM((2, B, 2, NZ), F32),
            pltpu.VMEM((2, shots, 2, APX // 2, 16, NZ), int16),
            pltpu.VMEM((2, shots, 2, NZ), F32),
            pltpu.VMEM((2, total, 2 * groups * NZ), BF16),
            pltpu.VMEM((2, 2, shots * positions, 2 * NZ), BF16),
            pltpu.VMEM((2, total, 2 * NZ), int16),
            pltpu.VMEM((2, across, 8, rows), F32),
            pltpu.VMEM((2, across, rows, 2 * NZ), int16),
            pltpu.VMEM((2, across, 8, rows), F32),
            pltpu.VMEM((2, rows, 2 * NZ), F32),
            pltpu.VMEM((2, depths, owned, 2 * NZ), F32),
            dma((depths,)), dma((depths,)),
            dma((2, across)), dma((2, across)),
            dma((2, shots)), dma((2, shots)), dma((2, shots)), dma((2, shots)),
            dma((2, shots)), dma((2, shots)), dma((2, shots)), dma((2, shots)),
            dma((2, across)), dma((2, across)), dma((2, across)), dma((2, across)),
            dma((2, depths)), dma((2, depths)),
        ],
        compiler_params=pltpu.CompilerParams(
            collective_id=0, has_side_effects=True, vmem_limit_bytes=56 * 1024 * 1024
        ),
        cost_estimate=pl.CostEstimate(flops=2 * 10**9, bytes_accessed=5 * 2**20, transcendentals=0),
        name="shot_gradients",
    )(
        tile_store, aperture, model, source, pulses, cells, traces, fwd, adj,
        jnp.asarray(depth.astype(np.float32)), jnp.asarray(middle.astype(np.float32)),
    )


def per_device(
    tile_store, apertures, model, fwd_states, adj_states, source_cell, wavelet, receiver_cells, residuals
):
    shots, tiles = lax.axis_size("shot"), lax.axis_size("tile")
    owned = model.shape[0]
    sums = shot_gradients(
        tile_store.reshape(1, -1), apertures, model.reshape(owned, -1), source_cell, wavelet,
        receiver_cells, residuals[0], fwd_states, adj_states, shots, tiles,
    )
    return sums.reshape(owned, 2, -1)


def solution(mesh):
    return jax.shard_map(
        per_device,
        mesh=mesh,
        in_specs=(
            P(),
            P(("shot", "tile"), None),
            P("tile", None, None),
            P(("shot", "tile"), None, None, None, None),
            P(("shot", "tile"), None, None, None, None),
            P(("shot", "tile")),
            P(("shot", "tile"), None),
            P(("shot", "tile"), None),
            P(("shot", "tile"), None, None),
        ),
        out_specs=P("tile", None, "shot"),
        check_vma=False,
    )
```

```python
import jax
import jax.numpy as jnp
import ml_dtypes
import numpy as np
from jax import lax
from jax.experimental import pallas as pl
from jax.experimental.pallas import tpu as pltpu
from jax.sharding import PartitionSpec as P

B = 16
APX = 4
APZ = 8
NX, NY, NZ = 64, 16, 128
STEPS = 8
NREC = 256
COEF_SECOND = (-205.0 / 72.0, 8.0 / 5.0, -1.0 / 5.0, 8.0 / 315.0, -1.0 / 560.0)
COEF_FIRST = (4.0 / 5.0, -1.0 / 5.0, 4.0 / 105.0, -1.0 / 280.0)
SPEED_SCALE = 0.12
F32 = jnp.float32
BF16 = jnp.bfloat16
LEVELS = 32767.0
SMALLEST = 1e-30
MESH = pl.DeviceIdType.MESH
PLANES = 8
CHUNKS = NX // PLANES
ROWS = PLANES * NY
UNROLL = 8
DEPTH_CHIPS = 8
TURNED = tuple((8 - i) % 8 for i in range(8))


def band(extent, centre):
    second = np.zeros((extent, extent))
    first = np.zeros((extent, extent))
    for to in range(extent):
        second[to, to] = centre
        for reach in range(1, 5):
            if to + reach < extent:
                second[to, to + reach] = COEF_SECOND[reach]
                first[to, to + reach] = COEF_FIRST[reach - 1]
            if to - reach >= 0:
                second[to, to - reach] = COEF_SECOND[reach]
                first[to, to - reach] = -COEF_FIRST[reach - 1]
    return second, first


def parts_of(matrix):
    high = matrix.astype(ml_dtypes.bfloat16)
    low = (matrix - high.astype(np.float64)).astype(ml_dtypes.bfloat16)
    return high, low


def depth_matrix():
    second, first = band(NZ, 3.0 * COEF_SECOND[0])
    high, low = parts_of(np.concatenate([second.T, first.T], axis=1))
    return np.concatenate([high, high, low], axis=0)


def middle_matrix():
    second, first = band(NY, 0.0)
    eight = np.eye(PLANES)
    both = np.stack([np.kron(eight, second), np.kron(eight, first)])
    both = both.reshape(2, PLANES * 2, 8, ROWS).transpose(1, 0, 2, 3).reshape(2 * ROWS, ROWS)
    high, low = parts_of(both)
    return np.concatenate([high, high, low], axis=1)


def split_two(values):
    high = values.astype(BF16)
    low = (values - high.astype(F32)).astype(BF16)
    return high, low


def to_levels(values):
    return jnp.round(values).astype(jnp.int32).astype(jnp.int16)


def turn(block, lane_block):
    block = pltpu.roll(block, 0, 1, stride=B, stride_axis=0)
    for bit in (1, 2, 4):
        block = jnp.where((lane_block & bit) != 0, pltpu.roll(block, 8 - bit, 0), block)
    return pltpu.roll(block, 0, 1, stride=B, stride_axis=0)


def products(window_ref, at, depth_ref, middle_ref):
    inner = window_ref[pl.ds(at * PLANES + 4, PLANES)].reshape(ROWS, NZ)
    high, low = split_two(inner)
    along_depth = jnp.dot(
        jnp.concatenate([high, low, high], axis=1), depth_ref[...], preferred_element_type=F32
    )
    along_middle = jnp.dot(
        middle_ref[...], jnp.concatenate([high, low, high], axis=0), preferred_element_type=F32
    )
    return along_depth, along_middle


def each_block(window_ref, at, depth_ref, middle_ref, body):
    along_depth, along_middle = products(window_ref, at, depth_ref, middle_ref)
    base = at * PLANES
    window = [[window_ref[base + j, 8 * half : 8 * half + 8] for half in range(2)] for j in range(8)]
    for plane in range(PLANES):
        window.append([window_ref[base + plane + 8, 8 * half : 8 * half + 8] for half in range(2)])
        for half in range(2):
            row = (plane * 2 + half) * 8
            second = along_depth[row : row + 8, :NZ] + along_middle[2 * row : 2 * row + 8]
            first = None
            for reach in range(1, 5):
                ahead, behind = window[plane + 4 + reach][half], window[plane + 4 - reach][half]
                second = second + COEF_SECOND[reach] * (ahead + behind)
                term = COEF_FIRST[reach - 1] * (ahead - behind)
                first = term if first is None else first + term
            body(
                base + plane, slice(8 * half, 8 * half + 8), window[plane + 4][half],
                second, first, along_middle[2 * row + 8 : 2 * row + 16], along_depth[row : row + 8, NZ:],
            )


def place():
    shot, tile = lax.axis_index("shot"), lax.axis_index("tile")
    return lax.div(shot, 2), lax.rem(shot, 2), lax.div(tile, DEPTH_CHIPS), lax.rem(tile, DEPTH_CHIPS)


def shifted(index, by, size):
    return lax.rem(index + by, size)


def near_first(i, size):
    return jnp.where(lax.rem(i, 2) == 1, lax.div(i + 1, 2), size - lax.div(i, 2))


def chunk_of(route, index, y):
    if route == 0:
        return index
    return lax.rem(3 * y + lax.div(index, 2), DEPTH_CHIPS) * 2 + lax.rem(index, 2)


def greet(y, core, x, z, shots, across, depths):
    barrier = pltpu.get_barrier_semaphore()
    shot, turned_shot = y * 2 + core, z * 2 + core

    def signal(device_id):
        pl.semaphore_signal(barrier, inc=1, device_id=device_id, device_id_type=MESH)

    for by in range(1, depths):
        signal((shot, x * depths + shifted(z, by, depths)))
    for by in range(1, across):
        signal((shot, shifted(x, by, across) * depths + z))

    def to_columns(by, carry):
        signal((shifted(shot, by, shots), x * depths + z))
        other = shifted(turned_shot, by, shots)
        signal((y * 2 + lax.rem(other, 2), x * depths + lax.div(other, 2)))
        return carry

    lax.fori_loop(1, shots, to_columns, 0)
    home = lax.rem(3 * y + z, depths)

    def to_last(from_y, carry):
        @pl.when(jnp.logical_or(from_y != y, home != y))
        def _():
            signal((from_y * 2 + core, x * depths + lax.rem(y + 3 * depths - 3 * from_y, depths)))

        return carry

    lax.fori_loop(0, depths, to_last, 0)
    here = jnp.where(home == y, 1, 0)
    return barrier, 2 * (shots - 1) + across - 1 + depths - 1 + depths - here


def remote(src, dst, send_sem, recv_sem, device_id):
    return pltpu.make_async_remote_copy(
        src_ref=src, dst_ref=dst, send_sem=send_sem, recv_sem=recv_sem,
        device_id=device_id, device_id_type=MESH,
    )


def rows_at(start, size):
    return pl.ds(pl.multiple_of(start, size), size)


def row_levels(values):
    rows, lanes = values.shape
    lane = lax.broadcasted_iota(jnp.int32, (rows, NZ), 1)
    coded, units = [], jnp.zeros((rows, NZ), F32)
    for at in range(lanes // NZ):
        part = values[:, at * NZ : (at + 1) * NZ]
        largest = jnp.maximum(jnp.max(jnp.abs(part), axis=1, keepdims=True), SMALLEST)
        units = jnp.where(lane == at, largest * (1.0 / LEVELS), units)
        coded.append(part * (LEVELS / largest))
    return to_levels(jnp.concatenate(coded, axis=1)), jnp.transpose(units)[:8]


def from_levels(levels, units):
    values = levels.astype(F32)
    return jnp.concatenate(
        [values[:, at * NZ : (at + 1) * NZ] * units[:, at : at + 1] for at in range(values.shape[1] // NZ)],
        axis=1,
    )


def shot_kernel(
    tile_store_ref, aperture_ref, model_ref, source_ref, pulse_ref, cells_ref, traces_ref,
    fwd_hbm, adj_hbm, depth_hbm, middle_hbm,
    out_ref,
    depth_ref, middle_ref, depth_f32, middle_f32, load_sem,
    blocks_ref, names_ref, store_ref, pick_ref, names_all, outgoing, incoming,
    gain_ref, speed_ref, slope_ref, wave_ref, adj_ref, image_ref, first_ref, inject_ref, hot_ref,
    mask_ref, sums_ref,
    grads_ref, units_ref, grads_all, units_all, place_ref, spread_ref,
    whole_levels, whole_lines, from_x, lines_x, column, from_z,
    z_send, z_recv, x_send, x_recv, name_send, name_recv, shot_send, shot_recv,
    grad_send, grad_recv, unit_send, unit_recv, gx_send, gx_recv, xu_send, xu_recv,
    gz_send, gz_recv,
):
    y, core, x, z = place()
    shots, across, depths = names_all.shape[1], from_x.shape[1], DEPTH_CHIPS
    owned = model_ref.shape[0]
    me = x * depths + z
    positions = APX * APZ
    group = NZ // positions
    total = store_ref.shape[0] * owned
    cells_of = model_ref.shape[1] // 2
    lane_block = lax.broadcasted_iota(jnp.int32, (8, NZ), 1) // B

    mine = (y * 2 + core, z * 2 + core)

    def on_route(route, index):
        if route == 0:
            return (index, me)
        return (y * 2 + lax.rem(index, 2), x * depths + lax.div(index, 2))

    loads = [
        pltpu.make_async_copy(src, dst, load_sem.at[i])
        for i, (src, dst) in enumerate(
            [
                (depth_hbm, depth_f32),
                (middle_hbm, middle_f32),
                (fwd_hbm.at[0, 0], wave_ref.at[0, pl.ds(4, NX)]),
                (fwd_hbm.at[0, 1], wave_ref.at[1, pl.ds(4, NX)]),
                (adj_hbm.at[0, 0], adj_ref.at[0, pl.ds(4, NX)]),
                (adj_hbm.at[0, 1], adj_ref.at[1, pl.ds(4, NX)]),
            ]
        )
    ]
    barrier, greeted = greet(y, core, x, z, shots, across, depths)
    for load in loads:
        load.start()

    from_lane = lax.broadcasted_iota(jnp.int32, (NZ, NZ), 0)
    to_lane = lax.broadcasted_iota(jnp.int32, (NZ, NZ), 1)
    mirror = (from_lane % B == to_lane % B) & (from_lane // B == (8 - to_lane // B) % 8)
    mirror = mirror.astype(F32).astype(BF16)

    def cut(chunk, route):
        parts = []
        for field in range(2):
            start = pl.multiple_of(field * cells_of + chunk * 2 * NZ + route * NZ, NZ)
            parts.append(model_ref[:, pl.ds(start, NZ)])
        return jnp.concatenate(parts, axis=0)

    cuts = [cut(mine[0], 0)] + [
        cut(chunk_of(1, to * 2 + core, y), 1) for to in range(depths)
    ]
    mirrored = jnp.dot(jnp.concatenate(cuts, axis=0), mirror, preferred_element_type=F32).astype(BF16)
    for to in range(depths):
        for route in range(2):
            for field in range(2):
                row = ((route * (to + 1)) * 2 + field) * owned
                blocks_ref[to, route, :, field * NZ : field * NZ + NZ] = mirrored[row : row + owned]

    wanted = jnp.concatenate([aperture_ref[...]] * group, axis=1)
    tile_ids = lax.broadcasted_iota(jnp.int32, (total, NZ), 0)
    chosen = (tile_ids == wanted).astype(F32).astype(BF16)
    digits = jnp.broadcast_to(tile_store_ref[...], (8, total))
    digit_row = lax.broadcasted_iota(jnp.int32, (8, total), 0)
    digits = jnp.where(digit_row == 0, lax.shift_right_logical(digits, 4), digits & 15)
    found = jnp.dot(digits.astype(F32).astype(BF16), chosen, preferred_element_type=F32)
    turn_lanes = (from_lane // 8 == to_lane // 8) & (from_lane % 8 == (8 - to_lane % 8) % 8)
    found_turned = jnp.dot(
        found.astype(BF16), turn_lanes.astype(F32).astype(BF16), preferred_element_type=F32
    )
    lane_group = lax.broadcasted_iota(jnp.int32, (1, NZ), 1) // positions
    for route in range(2):
        member = lane_group == lax.rem(mine[route], group)
        for kind, digits_of in enumerate((found, found_turned)):
            line = 16.0 * digits_of[0:1] + digits_of[1:2]
            names_ref[2 * route + kind : 2 * route + kind + 1] = jnp.where(member, line, 0.0)

    pl.semaphore_wait(barrier, greeted)

    store_ref[me] = blocks_ref[z]
    for route in range(2):
        names_all[route, mine[route]] = names_ref[...]

    def z_copy(by):
        target = shifted(z, by, depths)
        return remote(
            blocks_ref.at[target], store_ref.at[me],
            z_send.at[by], z_recv.at[by], (mine[0], x * depths + target),
        )

    def name_copy(route, by):
        return remote(
            names_ref, names_all.at[route, mine[route]],
            name_send.at[route, by], name_recv.at[route, by],
            on_route(route, shifted(mine[route], by, shots)),
        )

    def x_copy(route, along):
        part = store_ref.at[pl.ds(x * depths, depths), route]
        return remote(
            part, part, x_send.at[route, along], x_recv.at[route, along],
            (mine[0], shifted(x, along, across) * depths + z),
        )

    def start_z(by, carry):
        z_copy(by).start()
        return carry

    def start_name(by, carry):
        for route in range(2):
            name_copy(route, by).start()
        return carry

    def wait_z(by, carry):
        z_copy(by).wait_recv()
        return carry

    lax.fori_loop(1, depths, start_z, 0)
    lax.fori_loop(1, shots, start_name, 0)
    lax.fori_loop(1, depths, wait_z, 0)
    for route in range(2):
        for along in (2, 1, 3):
            x_copy(route, along).start()

    def wait_name(by, carry):
        for route in range(2):
            name_copy(route, by).wait_recv()
        return carry

    lax.fori_loop(1, shots, wait_name, 0)

    groups = shots // group
    lines = [
        sum(names_all[route, group * at + i, 2 * route : 2 * route + 1] for i in range(group))
        for route in range(2)
        for at in range(groups)
    ]
    columns = jnp.transpose(jnp.concatenate(lines, axis=0))
    row_ids = lax.broadcasted_iota(jnp.int32, (NZ, total), 1).astype(F32)
    for route in range(2):
        for at in range(groups):
            column_at = route * groups + at
            hot = (row_ids == columns[:, column_at : column_at + 1]).astype(F32).astype(BF16)
            pick_ref[route, at * NZ : at * NZ + NZ] = hot

    def shot_copy(route, by):
        target = shifted(mine[route], by, shots)
        return remote(
            outgoing.at[route, target], incoming.at[route, mine[route]],
            shot_send.at[route, by], shot_recv.at[route, by], on_route(route, target),
        )

    for route in range(2):
        for along in (1, 3, 2):
            x_copy(route, along).wait_recv()
        held = store_ref[:, route].reshape(total, 2 * NZ)
        picked = jnp.dot(pick_ref[route], held, preferred_element_type=F32)
        outgoing[route] = picked.astype(BF16).reshape(shots, positions, 2 * NZ)

        def start_shot(i, carry):
            shot_copy(route, near_first(shots - i, shots)).start()
            return carry

        lax.fori_loop(1, shots, start_shot, 0)
    for route in range(2):
        incoming[route, mine[route]] = outgoing[route, mine[route]]

    for load in loads:
        load.wait()
    depth_ref[...] = depth_f32[...].astype(BF16)
    middle_ref[...] = middle_f32[...].astype(BF16)
    border = jnp.zeros((4, NY, NZ), F32)
    for ref in (gain_ref, wave_ref.at[0], wave_ref.at[1], adj_ref.at[0], adj_ref.at[1]):
        ref[0:4] = border
        ref[NX + 4 : NX + 8] = border

    source = source_ref[0]
    lane_ids = lax.broadcasted_iota(jnp.int32, (NY, NZ), 1)
    row_of = lax.broadcasted_iota(jnp.int32, (NY, NZ), 0)

    def mark(plane, carry):
        cell = (plane * NY + row_of) * NZ + lane_ids
        mask_ref[plane] = (cell == source).astype(F32)
        sums_ref[1, plane] = jnp.zeros((NY, NZ), F32)
        return carry

    lax.fori_loop(0, NX, mark, 0)

    cells = cells_ref[...]
    cell_rows = lax.shift_right_logical(cells, 7)
    cell_lanes = jnp.transpose(jnp.broadcast_to((cells & 127).astype(F32), (8, NREC)))[:, 0:1]
    trace_columns = jnp.transpose(traces_ref[...])
    for at in range(8):
        row_ids = lax.broadcasted_iota(jnp.int32, (128, NREC), 0) + at * 128
        hot_ref[at * 128 : at * 128 + 128] = (row_ids == cell_rows).astype(F32).astype(BF16)
    lane_hot = lax.broadcasted_iota(jnp.int32, (NREC, NZ), 1).astype(F32) == cell_lanes
    for step in range(STEPS):
        high, low = split_two(jnp.where(lane_hot, trace_columns[:, step : step + 1], 0.0))
        both = jnp.concatenate([high, low], axis=1)
        added = jnp.dot(hot_ref[...], both, preferred_element_type=F32)
        inject_ref[step] = (added[:, :NZ] + added[:, NZ:]).reshape(NX, NY, NZ)

    store_rows = lax.broadcasted_iota(jnp.int32, (total, NZ), 0).astype(F32)
    for route in range(2):
        for at in range(groups):
            line = sum(names_all[route, group * at + i, 2 * route + 1 : 2 * route + 2] for i in range(group))
            hot = (store_rows == line).astype(F32).astype(BF16)
            for part in range(2):
                lanes = (part * groups + at) * NZ
                place_ref[route, :, lanes : lanes + NZ] = hot

    def unpack(route, by):
        sender = shifted(mine[route], shots - by, shots)
        plane = chunk_of(route, sender, y)
        for block in range(APX):
            at = block * B + plane
            for field in range(2):
                part = incoming[route, sender, block * 8 : block * 8 + 8, field * NZ : field * NZ + NZ]
                turned = turn(part.astype(F32), lane_block)
                if field == 0:
                    speed_ref[at, 8 * route : 8 * route + 8] = SPEED_SCALE * turned
                else:
                    gain_ref[at + 4, 8 * route : 8 * route + 8] = turned

    def arrived(i, carry):
        by = near_first(i, shots)
        for route in range(2):
            shot_copy(route, by).wait_recv()
            unpack(route, by)
        return carry

    for route in range(2):
        unpack(route, 0)
    lax.fori_loop(1, shots, arrived, 0)

    def run(window_ref, body):
        def chunk(at, carry):
            each_block(window_ref, at, depth_ref, middle_ref, body)
            return carry

        lax.fori_loop(0, CHUNKS, chunk, 0, unroll=UNROLL)

    def slopes(plane, rows, centre, second, *firsts):
        for axis in range(3):
            slope_ref[axis, plane, rows] = firsts[axis]

    run(gain_ref, slopes)

    def apply(plane, rows, second, firsts):
        applied = gain_ref[plane + 4, rows] * second
        for axis in range(3):
            applied = applied + slope_ref[axis, plane, rows] * firsts[axis]
        return applied

    def forward(step, now_ref, other_ref):
        pulse = pulse_ref[0, step]

        def body(plane, rows, centre, second, *firsts):
            applied = apply(plane, rows, second, firsts)
            image_ref[step, plane, rows] = applied
            for axis in range(3):
                first_ref[step, axis, plane, rows] = firsts[axis]
            newer = 2.0 * centre - other_ref[plane + 4, rows] + speed_ref[plane, rows] * applied
            other_ref[plane + 4, rows] = newer + pulse * mask_ref[plane, rows]

        run(now_ref, body)

    def forward_pair(pair, carry):
        forward(2 * pair, wave_ref.at[1], wave_ref.at[0])
        forward(2 * pair + 1, wave_ref.at[0], wave_ref.at[1])
        return carry

    lax.fori_loop(0, STEPS // 2, forward_pair, 0)

    def backward(step, now_ref, other_ref, start):
        def body(plane, rows, centre, second, *firsts):
            applied = apply(plane, rows, second, firsts)
            newer = 2.0 * centre - other_ref[plane + 4, rows] + speed_ref[plane, rows] * applied
            newer = newer + inject_ref[step, plane, rows]
            other_ref[plane + 4, rows] = newer
            part = newer * image_ref[step, plane, rows]
            if start:
                sums_ref[0, plane, rows] = part
            else:
                sums_ref[0, plane, rows] = sums_ref[0, plane, rows] + part
                part = firsts[0] * first_ref[step + 1, 0, plane, rows]
                part = part + firsts[1] * first_ref[step + 1, 1, plane, rows]
                part = part + firsts[2] * first_ref[step + 1, 2, plane, rows]
                sums_ref[1, plane, rows] = sums_ref[1, plane, rows] + part

        run(now_ref, body)

    backward(STEPS - 1, adj_ref.at[1], adj_ref.at[0], True)

    def backward_pair(pair, carry):
        backward(STEPS - 2 - 2 * pair, adj_ref.at[0], adj_ref.at[1], False)
        backward(STEPS - 3 - 2 * pair, adj_ref.at[1], adj_ref.at[0], False)
        return carry

    lax.fori_loop(0, STEPS // 2 - 1, backward_pair, 0)
    backward(0, adj_ref.at[0], adj_ref.at[1], False)

    def last(plane, rows, centre, second, *firsts):
        part = sums_ref[1, plane, rows]
        for axis in range(3):
            part = part + firsts[axis] * first_ref[0, axis, plane, rows]
        sums_ref[1, plane, rows] = part * speed_ref[plane, rows]

    run(adj_ref.at[1], last)

    def code(route, index):
        plane = chunk_of(route, index, y)
        for field in range(2):
            values = [
                sums_ref[field, block * B + plane, 8 * route : 8 * route + 8] for block in range(APX)
            ]
            largest = jnp.abs(values[0])
            for value in values[1:]:
                largest = jnp.maximum(largest, jnp.abs(value))
            largest = jnp.maximum(jnp.max(largest, axis=(0, 1), keepdims=True), SMALLEST)
            units_ref[route, index, field : field + 1] = jnp.broadcast_to(largest * (1.0 / LEVELS), (1, NZ))
            levels = LEVELS / largest
            for pair in range(APX // 2):
                both = jnp.concatenate(values[2 * pair : 2 * pair + 2], axis=0)
                grads_ref[route, index, field, pair] = to_levels(both * levels)

    def grad_copy(route, by):
        target = shifted(mine[route], by, shots)
        return remote(
            grads_ref.at[route, target], grads_all.at[route, mine[route]],
            grad_send.at[route, by], grad_recv.at[route, by], on_route(route, target),
        )

    def unit_copy(route, by):
        target = shifted(mine[route], by, shots)
        return remote(
            units_ref.at[route, target], units_all.at[route, mine[route]],
            unit_send.at[route, by], unit_recv.at[route, by], on_route(route, target),
        )

    def start_grad(i, carry):
        by = near_first(shots - i, shots)
        for route in range(2):
            code(route, shifted(mine[route], by, shots))
            grad_copy(route, by).start()
            unit_copy(route, by).start()
        return carry

    lax.fori_loop(1, shots, start_grad, 0)
    for route in range(2):
        code(route, mine[route])
        grads_all[route, mine[route]] = grads_ref[route, mine[route]]
        units_all[route, mine[route]] = units_ref[route, mine[route]]

    def spread(route, by):
        sender = shifted(mine[route], shots - by, shots)
        for field in range(2):
            unit = units_all[route, sender, field : field + 1]
            for pair in range(APX // 2):
                values = grads_all[route, sender, field, pair].astype(F32) * unit
                turned = [turn(values[8 * i : 8 * i + 8], lane_block) for i in range(2)]
                high, low = split_two(jnp.concatenate(turned, axis=0))
                rows = pl.ds(pl.multiple_of(sender * positions + pair * 16, 16), 16)
                spread_ref[route, 0, rows, field * NZ : field * NZ + NZ] = high
                spread_ref[route, 1, rows, field * NZ : field * NZ + NZ] = low

    block = depths * owned

    def gx_copy(route, along):
        target = shifted(x, along, across)
        return remote(
            whole_levels.at[route, rows_at(target * block, block)], from_x.at[route, along],
            gx_send.at[route, along], gx_recv.at[route, along], (mine[0], target * depths + z),
        )

    def gx_lines(route, along):
        target = shifted(x, along, across)
        return remote(
            whole_lines.at[route, target], lines_x.at[route, along],
            xu_send.at[route, along], xu_recv.at[route, along], (mine[0], target * depths + z),
        )

    def merge(route, along):
        target = shifted(x, along, across)
        rows = rows_at(target * block, block)
        parts = spread_ref[route].reshape(2 * shots * positions, 2 * NZ)
        added = jnp.dot(place_ref[route, rows], parts, preferred_element_type=F32)
        if along == 0:
            column[route] = added
            return
        coded, units = row_levels(added)
        whole_levels[route, rows] = coded
        whole_lines[route, target] = units
        gx_copy(route, along).start()
        gx_lines(route, along).start()

    for route in range(2):
        spread(route, 0)
    for route in range(2):

        def returned(i, carry):
            by = near_first(i, shots)
            grad_copy(route, by).wait_recv()
            unit_copy(route, by).wait_recv()
            spread(route, by)
            return carry

        lax.fori_loop(1, shots, returned, 0)
        for along in (2, 1, 3):
            merge(route, along)
    for route in range(2):
        merge(route, 0)

    def sum_x(route):
        summed = column[route]
        for along in (1, 3, 2):
            gx_copy(route, along).wait_recv()
            gx_lines(route, along).wait_recv()
            summed = summed + from_levels(from_x[route, along], jnp.transpose(lines_x[route, along]))
        column[route] = summed

    home = lax.rem(3 * y + z, depths)

    def gz_copy(by):
        target = shifted(z, by, depths)
        return remote(
            column.at[0, rows_at(target * owned, owned)], from_z.at[0, by],
            gz_send.at[0, by], gz_recv.at[0, by], (mine[0], x * depths + target),
        )

    def gy_copy(by):
        target = shifted(z, by, depths)
        return remote(
            column.at[1, rows_at(target * owned, owned)], from_z.at[1, y],
            gz_send.at[1, by], gz_recv.at[1, y], (home * 2 + core, x * depths + target),
        )

    def gy_arrival(from_y):
        return remote(
            column.at[1, rows_at(z * owned, owned)], from_z.at[1, from_y],
            gz_send.at[1, 0], gz_recv.at[1, from_y], (home * 2 + core, x * depths + shifted(z, 1, depths)),
        )

    def start_gz(by, carry):
        gz_copy(by).start()
        return carry

    def start_gy(by, carry):
        gy_copy(by).start()
        return carry

    sum_x(0)
    lax.fori_loop(1, depths, start_gz, 0)
    sum_x(1)
    lax.fori_loop(1, depths, start_gy, 0)

    @pl.when(home != y)
    def _():
        gy_copy(0).start()

    from_z[0, 0] = column[0, rows_at(z * owned, owned)]

    @pl.when(home == y)
    def _():
        from_z[1, y] = column[1, rows_at(z * owned, owned)]

    def end_z(by, carry):
        gz_copy(by).wait_recv()
        return carry

    def end_y(from_y, carry):
        @pl.when(jnp.logical_or(from_y != y, home != y))
        def _():
            gy_arrival(from_y).wait_recv()

        return carry

    lax.fori_loop(1, depths, end_z, 0)
    lax.fori_loop(0, depths, end_y, 0)
    for route in range(2):
        ended = from_z[route, 0]
        for by in range(1, depths):
            ended = ended + from_z[route, by]
        for field in range(2):
            lanes = (2 * field + route) * NZ
            out_ref[:, lanes : lanes + NZ] = ended[:, field * NZ : field * NZ + NZ]

    def finish_shots(by, carry):
        for route in range(2):
            shot_copy(route, by).wait_send()
            name_copy(route, by).wait_send()
            grad_copy(route, by).wait_send()
            unit_copy(route, by).wait_send()
        return carry

    def finish_z(by, carry):
        z_copy(by).wait_send()
        gz_copy(by).wait_send()
        gy_copy(by).wait_send()
        return carry

    lax.fori_loop(1, shots, finish_shots, 0)
    lax.fori_loop(1, depths, finish_z, 0)
    for route in range(2):
        for along in range(1, across):
            x_copy(route, along).wait_send()
            gx_copy(route, along).wait_send()
            gx_lines(route, along).wait_send()

    @pl.when(home != y)
    def _():
        gy_copy(0).wait_send()


def shot_gradients(tile_store, aperture, model, source, pulses, cells, traces, fwd, adj, shots, tiles):
    vmem = pl.BlockSpec(memory_space=pltpu.VMEM)
    smem = pl.BlockSpec(memory_space=pltpu.SMEM)
    hbm = pl.BlockSpec(memory_space=pltpu.HBM)
    owned = model.shape[0]
    lanes = model.shape[1] // shots
    depths = DEPTH_CHIPS
    across = tiles // depths
    total = tiles * owned
    positions = APX * APZ
    groups = shots * positions // NZ
    rows = depths * owned
    volume = (NX, NY, NZ)
    padded = (NX + 8, NY, NZ)
    int16 = jnp.int16
    dma = pltpu.SemaphoreType.DMA
    depth, middle = depth_matrix(), middle_matrix()
    return pl.pallas_call(
        shot_kernel,
        out_shape=jax.ShapeDtypeStruct((owned, lanes), F32),
        in_specs=[vmem, vmem, vmem, smem, smem, vmem, vmem, hbm, hbm, hbm, hbm],
        out_specs=vmem,
        scratch_shapes=[
            pltpu.VMEM(depth.shape, BF16),
            pltpu.VMEM(middle.shape, BF16),
            pltpu.VMEM(depth.shape, F32),
            pltpu.VMEM(middle.shape, F32),
            dma((6,)),
            pltpu.VMEM((depths, 2, owned, 2 * NZ), BF16),
            pltpu.VMEM((8, NZ), F32),
            pltpu.VMEM((tiles, 2, owned, 2 * NZ), BF16),
            pltpu.VMEM((2, shots * positions, total), BF16),
            pltpu.VMEM((2, shots, 8, NZ), F32),
            pltpu.VMEM((2, shots, positions, 2 * NZ), BF16),
            pltpu.VMEM((2, shots, positions, 2 * NZ), BF16),
            pltpu.VMEM(padded, F32),
            pltpu.VMEM(volume, F32),
            pltpu.VMEM((3,) + volume, F32),
            pltpu.VMEM((2,) + padded, F32),
            pltpu.VMEM((2,) + padded, F32),
            pltpu.VMEM((STEPS,) + volume, F32),
            pltpu.VMEM((STEPS, 3) + volume, F32),
            pltpu.VMEM((STEPS,) + volume, F32),
            pltpu.VMEM((NX * NY, NREC), BF16),
            pltpu.VMEM(volume, F32),
            pltpu.VMEM((2,) + volume, F32),
            pltpu.VMEM((2, B, 2, APX // 2, 16, NZ), int16),
            pltpu.VMEM((2, B, 2, NZ), F32),
            pltpu.VMEM((2, shots, 2, APX // 2, 16, NZ), int16),
            pltpu.VMEM((2, shots, 2, NZ), F32),
            pltpu.VMEM((2, total, 2 * groups * NZ), BF16),
            pltpu.VMEM((2, 2, shots * positions, 2 * NZ), BF16),
            pltpu.VMEM((2, total, 2 * NZ), int16),
            pltpu.VMEM((2, across, 8, rows), F32),
            pltpu.VMEM((2, across, rows, 2 * NZ), int16),
            pltpu.VMEM((2, across, 8, rows), F32),
            pltpu.VMEM((2, rows, 2 * NZ), F32),
            pltpu.VMEM((2, depths, owned, 2 * NZ), F32),
            dma((depths,)), dma((depths,)),
            dma((2, across)), dma((2, across)),
            dma((2, shots)), dma((2, shots)), dma((2, shots)), dma((2, shots)),
            dma((2, shots)), dma((2, shots)), dma((2, shots)), dma((2, shots)),
            dma((2, across)), dma((2, across)), dma((2, across)), dma((2, across)),
            dma((2, depths)), dma((2, depths)),
        ],
        compiler_params=pltpu.CompilerParams(
            collective_id=0, has_side_effects=True, vmem_limit_bytes=56 * 1024 * 1024
        ),
        cost_estimate=pl.CostEstimate(flops=2 * 10**9, bytes_accessed=5 * 2**20, transcendentals=0),
        name="shot_gradients",
    )(
        tile_store, aperture, model, source, pulses, cells, traces, fwd, adj,
        jnp.asarray(depth.astype(np.float32)), jnp.asarray(middle.astype(np.float32)),
    )


def per_device(
    tile_store, apertures, model, fwd_states, adj_states, source_cell, wavelet, receiver_cells, residuals
):
    shots, tiles = lax.axis_size("shot"), lax.axis_size("tile")
    owned = model.shape[0]
    sums = shot_gradients(
        tile_store.reshape(1, -1), apertures, model.reshape(owned, -1), source_cell, wavelet,
        receiver_cells, residuals[0], fwd_states, adj_states, shots, tiles,
    )
    return sums.reshape(owned, 2, -1)


def solution(mesh):
    return jax.shard_map(
        per_device,
        mesh=mesh,
        in_specs=(
            P(),
            P(("shot", "tile"), None),
            P("tile", None, None),
            P(("shot", "tile"), None, None, None, None),
            P(("shot", "tile"), None, None, None, None),
            P(("shot", "tile")),
            P(("shot", "tile"), None),
            P(("shot", "tile"), None),
            P(("shot", "tile"), None, None),
        ),
        out_specs=P("tile", None, "shot"),
        check_vma=False,
    )
```

```python
import jax
import jax.numpy as jnp
import ml_dtypes
import numpy as np
from jax import lax
from jax.experimental import pallas as pl
from jax.experimental.pallas import tpu as pltpu
from jax.sharding import PartitionSpec as P

B = 16
APX = 4
APZ = 8
NX, NY, NZ = 64, 16, 128
STEPS = 8
NREC = 256
COEF_SECOND = (-205.0 / 72.0, 8.0 / 5.0, -1.0 / 5.0, 8.0 / 315.0, -1.0 / 560.0)
COEF_FIRST = (4.0 / 5.0, -1.0 / 5.0, 4.0 / 105.0, -1.0 / 280.0)
SPEED_SCALE = 0.12
F32 = jnp.float32
BF16 = jnp.bfloat16
LEVELS = 32767.0
SMALLEST = 1e-30
MESH = pl.DeviceIdType.MESH
PLANES = 8
CHUNKS = NX // PLANES
ROWS = PLANES * NY
UNROLL = 8
DEPTH_CHIPS = 8
TURNED = tuple((8 - i) % 8 for i in range(8))


def band(extent, centre):
    second = np.zeros((extent, extent))
    first = np.zeros((extent, extent))
    for to in range(extent):
        second[to, to] = centre
        for reach in range(1, 5):
            if to + reach < extent:
                second[to, to + reach] = COEF_SECOND[reach]
                first[to, to + reach] = COEF_FIRST[reach - 1]
            if to - reach >= 0:
                second[to, to - reach] = COEF_SECOND[reach]
                first[to, to - reach] = -COEF_FIRST[reach - 1]
    return second, first


def parts_of(matrix):
    high = matrix.astype(ml_dtypes.bfloat16)
    low = (matrix - high.astype(np.float64)).astype(ml_dtypes.bfloat16)
    return high, low


def depth_matrix():
    second, first = band(NZ, 3.0 * COEF_SECOND[0])
    high, low = parts_of(np.concatenate([second.T, first.T], axis=1))
    return np.concatenate([high, high, low], axis=0)


def middle_matrix():
    second, first = band(NY, 0.0)
    eight = np.eye(PLANES)
    both = np.stack([np.kron(eight, second), np.kron(eight, first)])
    both = both.reshape(2, PLANES * 2, 8, ROWS).transpose(1, 0, 2, 3).reshape(2 * ROWS, ROWS)
    high, low = parts_of(both)
    return np.concatenate([high, high, low], axis=1)


def split_two(values):
    high = values.astype(BF16)
    low = (values - high.astype(F32)).astype(BF16)
    return high, low


def to_levels(values):
    return jnp.round(values).astype(jnp.int32).astype(jnp.int16)


def turn(block, lane_block):
    block = pltpu.roll(block, 0, 1, stride=B, stride_axis=0)
    for bit in (1, 2, 4):
        block = jnp.where((lane_block & bit) != 0, pltpu.roll(block, 8 - bit, 0), block)
    return pltpu.roll(block, 0, 1, stride=B, stride_axis=0)


def products(window_ref, at, depth_ref, middle_ref):
    inner = window_ref[pl.ds(at * PLANES + 4, PLANES)].reshape(ROWS, NZ)
    high, low = split_two(inner)
    along_depth = jnp.dot(
        jnp.concatenate([high, low, high], axis=1), depth_ref[...], preferred_element_type=F32
    )
    along_middle = jnp.dot(
        middle_ref[...], jnp.concatenate([high, low, high], axis=0), preferred_element_type=F32
    )
    return along_depth, along_middle


def each_block(window_ref, at, depth_ref, middle_ref, body):
    along_depth, along_middle = products(window_ref, at, depth_ref, middle_ref)
    base = at * PLANES
    window = [[window_ref[base + j, 8 * half : 8 * half + 8] for half in range(2)] for j in range(8)]
    for plane in range(PLANES):
        window.append([window_ref[base + plane + 8, 8 * half : 8 * half + 8] for half in range(2)])
        for half in range(2):
            row = (plane * 2 + half) * 8
            second = along_depth[row : row + 8, :NZ] + along_middle[2 * row : 2 * row + 8]
            first = None
            for reach in range(1, 5):
                ahead, behind = window[plane + 4 + reach][half], window[plane + 4 - reach][half]
                second = second + COEF_SECOND[reach] * (ahead + behind)
                term = COEF_FIRST[reach - 1] * (ahead - behind)
                first = term if first is None else first + term
            body(
                base + plane, slice(8 * half, 8 * half + 8), window[plane + 4][half],
                second, first, along_middle[2 * row + 8 : 2 * row + 16], along_depth[row : row + 8, NZ:],
            )


def place():
    shot, tile = lax.axis_index("shot"), lax.axis_index("tile")
    return lax.div(shot, 2), lax.rem(shot, 2), lax.div(tile, DEPTH_CHIPS), lax.rem(tile, DEPTH_CHIPS)


def shifted(index, by, size):
    return lax.rem(index + by, size)


def near_first(i, size):
    return jnp.where(lax.rem(i, 2) == 1, lax.div(i + 1, 2), size - lax.div(i, 2))


def chunk_of(route, index, y):
    if route == 0:
        return index
    return lax.rem(3 * y + lax.div(index, 2), DEPTH_CHIPS) * 2 + lax.rem(index, 2)


def greet(y, core, x, z, shots, across, depths):
    barrier = pltpu.get_barrier_semaphore()
    shot, turned_shot = y * 2 + core, z * 2 + core

    def signal(device_id):
        pl.semaphore_signal(barrier, inc=1, device_id=device_id, device_id_type=MESH)

    for by in range(1, depths):
        signal((shot, x * depths + shifted(z, by, depths)))
    for by in range(1, across):
        signal((shot, shifted(x, by, across) * depths + z))

    def to_columns(by, carry):
        signal((shifted(shot, by, shots), x * depths + z))
        other = shifted(turned_shot, by, shots)
        signal((y * 2 + lax.rem(other, 2), x * depths + lax.div(other, 2)))
        return carry

    lax.fori_loop(1, shots, to_columns, 0)
    home = lax.rem(3 * y + z, depths)

    def to_last(from_y, carry):
        @pl.when(jnp.logical_or(from_y != y, home != y))
        def _():
            signal((from_y * 2 + core, x * depths + lax.rem(y + 3 * depths - 3 * from_y, depths)))

        return carry

    lax.fori_loop(0, depths, to_last, 0)
    here = jnp.where(home == y, 1, 0)
    return barrier, 2 * (shots - 1) + across - 1 + depths - 1 + depths - here


def remote(src, dst, send_sem, recv_sem, device_id):
    return pltpu.make_async_remote_copy(
        src_ref=src, dst_ref=dst, send_sem=send_sem, recv_sem=recv_sem,
        device_id=device_id, device_id_type=MESH,
    )


def rows_at(start, size):
    return pl.ds(pl.multiple_of(start, size), size)


def row_levels(values):
    rows, lanes = values.shape
    lane = lax.broadcasted_iota(jnp.int32, (rows, NZ), 1)
    coded, units = [], jnp.zeros((rows, NZ), F32)
    for at in range(lanes // NZ):
        part = values[:, at * NZ : (at + 1) * NZ]
        largest = jnp.maximum(jnp.max(jnp.abs(part), axis=1, keepdims=True), SMALLEST)
        units = jnp.where(lane == at, largest * (1.0 / LEVELS), units)
        coded.append(part * (LEVELS / largest))
    return to_levels(jnp.concatenate(coded, axis=1)), jnp.transpose(units)[:8]


def from_levels(levels, units):
    values = levels.astype(F32)
    return jnp.concatenate(
        [values[:, at * NZ : (at + 1) * NZ] * units[:, at : at + 1] for at in range(values.shape[1] // NZ)],
        axis=1,
    )


def shot_kernel(
    tile_store_ref, aperture_ref, model_ref, source_ref, pulse_ref, cells_ref, traces_ref,
    fwd_hbm, adj_hbm, depth_hbm, middle_hbm,
    out_ref,
    depth_ref, middle_ref, depth_f32, middle_f32, load_sem,
    blocks_ref, names_ref, store_ref, pick_ref, names_all, outgoing, incoming,
    gain_ref, speed_ref, slope_ref, wave_ref, adj_ref, image_ref, first_ref, inject_ref, hot_ref,
    mask_ref, sums_ref,
    grads_ref, units_ref, grads_all, units_all, place_ref, spread_ref,
    whole_levels, whole_lines, from_x, lines_x, column, from_z,
    z_send, z_recv, x_send, x_recv, name_send, name_recv, shot_send, shot_recv,
    grad_send, grad_recv, unit_send, unit_recv, gx_send, gx_recv, xu_send, xu_recv,
    gz_send, gz_recv,
):
    y, core, x, z = place()
    shots, across, depths = names_all.shape[1], from_x.shape[1], DEPTH_CHIPS
    owned = model_ref.shape[0]
    me = x * depths + z
    positions = APX * APZ
    group = NZ // positions
    total = store_ref.shape[0] * owned
    cells_of = model_ref.shape[1] // 2
    lane_block = lax.broadcasted_iota(jnp.int32, (8, NZ), 1) // B

    mine = (y * 2 + core, z * 2 + core)

    def on_route(route, index):
        if route == 0:
            return (index, me)
        return (y * 2 + lax.rem(index, 2), x * depths + lax.div(index, 2))

    loads = [
        pltpu.make_async_copy(src, dst, load_sem.at[i])
        for i, (src, dst) in enumerate(
            [
                (depth_hbm, depth_f32),
                (middle_hbm, middle_f32),
                (fwd_hbm.at[0, 0], wave_ref.at[0, pl.ds(4, NX)]),
                (fwd_hbm.at[0, 1], wave_ref.at[1, pl.ds(4, NX)]),
                (adj_hbm.at[0, 0], adj_ref.at[0, pl.ds(4, NX)]),
                (adj_hbm.at[0, 1], adj_ref.at[1, pl.ds(4, NX)]),
            ]
        )
    ]
    barrier, greeted = greet(y, core, x, z, shots, across, depths)
    for load in loads:
        load.start()

    from_lane = lax.broadcasted_iota(jnp.int32, (NZ, NZ), 0)
    to_lane = lax.broadcasted_iota(jnp.int32, (NZ, NZ), 1)
    mirror = (from_lane % B == to_lane % B) & (from_lane // B == (8 - to_lane // B) % 8)
    mirror = mirror.astype(F32).astype(BF16)

    def cut(chunk, route):
        parts = []
        for field in range(2):
            start = pl.multiple_of(field * cells_of + chunk * 2 * NZ + route * NZ, NZ)
            parts.append(model_ref[:, pl.ds(start, NZ)])
        return jnp.concatenate(parts, axis=0)

    cuts = [cut(mine[0], 0)] + [
        cut(chunk_of(1, to * 2 + core, y), 1) for to in range(depths)
    ]
    mirrored = jnp.dot(jnp.concatenate(cuts, axis=0), mirror, preferred_element_type=F32).astype(BF16)
    for to in range(depths):
        for route in range(2):
            for field in range(2):
                row = ((route * (to + 1)) * 2 + field) * owned
                blocks_ref[to, route, :, field * NZ : field * NZ + NZ] = mirrored[row : row + owned]

    wanted = jnp.concatenate([aperture_ref[...]] * group, axis=1)
    tile_ids = lax.broadcasted_iota(jnp.int32, (total, NZ), 0)
    chosen = (tile_ids == wanted).astype(F32).astype(BF16)
    digits = jnp.broadcast_to(tile_store_ref[...], (8, total))
    digit_row = lax.broadcasted_iota(jnp.int32, (8, total), 0)
    digits = jnp.where(digit_row == 0, lax.shift_right_logical(digits, 4), digits & 15)
    found = jnp.dot(digits.astype(F32).astype(BF16), chosen, preferred_element_type=F32)
    turn_lanes = (from_lane // 8 == to_lane // 8) & (from_lane % 8 == (8 - to_lane % 8) % 8)
    found_turned = jnp.dot(
        found.astype(BF16), turn_lanes.astype(F32).astype(BF16), preferred_element_type=F32
    )
    lane_group = lax.broadcasted_iota(jnp.int32, (1, NZ), 1) // positions
    for route in range(2):
        member = lane_group == lax.rem(mine[route], group)
        for kind, digits_of in enumerate((found, found_turned)):
            line = 16.0 * digits_of[0:1] + digits_of[1:2]
            names_ref[2 * route + kind : 2 * route + kind + 1] = jnp.where(member, line, 0.0)

    pl.semaphore_wait(barrier, greeted)

    store_ref[me] = blocks_ref[z]
    for route in range(2):
        names_all[route, mine[route]] = names_ref[...]

    def z_copy(by):
        target = shifted(z, by, depths)
        return remote(
            blocks_ref.at[target], store_ref.at[me],
            z_send.at[by], z_recv.at[by], (mine[0], x * depths + target),
        )

    def name_copy(route, by):
        return remote(
            names_ref, names_all.at[route, mine[route]],
            name_send.at[route, by], name_recv.at[route, by],
            on_route(route, shifted(mine[route], by, shots)),
        )

    def x_copy(route, along):
        part = store_ref.at[pl.ds(x * depths, depths), route]
        return remote(
            part, part, x_send.at[route, along], x_recv.at[route, along],
            (mine[0], shifted(x, along, across) * depths + z),
        )

    def start_z(by, carry):
        z_copy(by).start()
        return carry

    def start_name(by, carry):
        for route in range(2):
            name_copy(route, by).start()
        return carry

    def wait_z(by, carry):
        z_copy(by).wait_recv()
        return carry

    lax.fori_loop(1, depths, start_z, 0)
    lax.fori_loop(1, shots, start_name, 0)
    lax.fori_loop(1, depths, wait_z, 0)
    for route in range(2):
        for along in (2, 1, 3):
            x_copy(route, along).start()

    def wait_name(by, carry):
        for route in range(2):
            name_copy(route, by).wait_recv()
        return carry

    lax.fori_loop(1, shots, wait_name, 0)

    groups = shots // group
    lines = [
        sum(names_all[route, group * at + i, 2 * route : 2 * route + 1] for i in range(group))
        for route in range(2)
        for at in range(groups)
    ]
    columns = jnp.transpose(jnp.concatenate(lines, axis=0))
    row_ids = lax.broadcasted_iota(jnp.int32, (NZ, total), 1).astype(F32)
    for route in range(2):
        for at in range(groups):
            column_at = route * groups + at
            hot = (row_ids == columns[:, column_at : column_at + 1]).astype(F32).astype(BF16)
            pick_ref[route, at * NZ : at * NZ + NZ] = hot

    def shot_copy(route, by):
        target = shifted(mine[route], by, shots)
        return remote(
            outgoing.at[route, target], incoming.at[route, mine[route]],
            shot_send.at[route, by], shot_recv.at[route, by], on_route(route, target),
        )

    for route in range(2):
        for along in (1, 3, 2):
            x_copy(route, along).wait_recv()
        held = store_ref[:, route].reshape(total, 2 * NZ)
        picked = jnp.dot(pick_ref[route], held, preferred_element_type=F32)
        outgoing[route] = picked.astype(BF16).reshape(shots, positions, 2 * NZ)

        def start_shot(i, carry):
            shot_copy(route, near_first(shots - i, shots)).start()
            return carry

        lax.fori_loop(1, shots, start_shot, 0)
    for route in range(2):
        incoming[route, mine[route]] = outgoing[route, mine[route]]

    for load in loads:
        load.wait()
    depth_ref[...] = depth_f32[...].astype(BF16)
    middle_ref[...] = middle_f32[...].astype(BF16)
    border = jnp.zeros((4, NY, NZ), F32)
    for ref in (gain_ref, wave_ref.at[0], wave_ref.at[1], adj_ref.at[0], adj_ref.at[1]):
        ref[0:4] = border
        ref[NX + 4 : NX + 8] = border

    source = source_ref[0]
    lane_ids = lax.broadcasted_iota(jnp.int32, (NY, NZ), 1)
    row_of = lax.broadcasted_iota(jnp.int32, (NY, NZ), 0)

    def mark(plane, carry):
        cell = (plane * NY + row_of) * NZ + lane_ids
        mask_ref[plane] = (cell == source).astype(F32)
        sums_ref[1, plane] = jnp.zeros((NY, NZ), F32)
        return carry

    lax.fori_loop(0, NX, mark, 0)

    cells = cells_ref[...]
    cell_rows = lax.shift_right_logical(cells, 7)
    cell_lanes = jnp.transpose(jnp.broadcast_to((cells & 127).astype(F32), (8, NREC)))[:, 0:1]
    trace_columns = jnp.transpose(traces_ref[...])
    for at in range(8):
        row_ids = lax.broadcasted_iota(jnp.int32, (128, NREC), 0) + at * 128
        hot_ref[at * 128 : at * 128 + 128] = (row_ids == cell_rows).astype(F32).astype(BF16)
    lane_hot = lax.broadcasted_iota(jnp.int32, (NREC, NZ), 1).astype(F32) == cell_lanes
    for step in range(STEPS):
        high, low = split_two(jnp.where(lane_hot, trace_columns[:, step : step + 1], 0.0))
        both = jnp.concatenate([high, low], axis=1)
        added = jnp.dot(hot_ref[...], both, preferred_element_type=F32)
        inject_ref[step] = (added[:, :NZ] + added[:, NZ:]).reshape(NX, NY, NZ)

    store_rows = lax.broadcasted_iota(jnp.int32, (total, NZ), 0).astype(F32)
    for route in range(2):
        for at in range(groups):
            line = sum(names_all[route, group * at + i, 2 * route + 1 : 2 * route + 2] for i in range(group))
            hot = (store_rows == line).astype(F32).astype(BF16)
            for part in range(2):
                lanes = (part * groups + at) * NZ
                place_ref[route, :, lanes : lanes + NZ] = hot

    def unpack(route, by):
        sender = shifted(mine[route], shots - by, shots)
        plane = chunk_of(route, sender, y)
        for block in range(APX):
            at = block * B + plane
            for field in range(2):
                part = incoming[route, sender, block * 8 : block * 8 + 8, field * NZ : field * NZ + NZ]
                turned = turn(part.astype(F32), lane_block)
                if field == 0:
                    speed_ref[at, 8 * route : 8 * route + 8] = SPEED_SCALE * turned
                else:
                    gain_ref[at + 4, 8 * route : 8 * route + 8] = turned

    def arrived(i, carry):
        by = near_first(i, shots)
        for route in range(2):
            shot_copy(route, by).wait_recv()
            unpack(route, by)
        return carry

    for route in range(2):
        unpack(route, 0)
    lax.fori_loop(1, shots, arrived, 0)

    def run(window_ref, body):
        def chunk(at, carry):
            each_block(window_ref, at, depth_ref, middle_ref, body)
            return carry

        lax.fori_loop(0, CHUNKS, chunk, 0, unroll=UNROLL)

    def slopes(plane, rows, centre, second, *firsts):
        for axis in range(3):
            slope_ref[axis, plane, rows] = firsts[axis]

    run(gain_ref, slopes)

    def apply(plane, rows, second, firsts):
        applied = gain_ref[plane + 4, rows] * second
        for axis in range(3):
            applied = applied + slope_ref[axis, plane, rows] * firsts[axis]
        return applied

    def forward(step, now_ref, other_ref):
        pulse = pulse_ref[0, step]

        def body(plane, rows, centre, second, *firsts):
            applied = apply(plane, rows, second, firsts)
            image_ref[step, plane, rows] = applied
            for axis in range(3):
                first_ref[step, axis, plane, rows] = firsts[axis]
            newer = 2.0 * centre - other_ref[plane + 4, rows] + speed_ref[plane, rows] * applied
            other_ref[plane + 4, rows] = newer + pulse * mask_ref[plane, rows]

        run(now_ref, body)

    def forward_pair(pair, carry):
        forward(2 * pair, wave_ref.at[1], wave_ref.at[0])
        forward(2 * pair + 1, wave_ref.at[0], wave_ref.at[1])
        return carry

    lax.fori_loop(0, STEPS // 2, forward_pair, 0)

    def backward(step, now_ref, other_ref, start):
        def body(plane, rows, centre, second, *firsts):
            applied = apply(plane, rows, second, firsts)
            newer = 2.0 * centre - other_ref[plane + 4, rows] + speed_ref[plane, rows] * applied
            newer = newer + inject_ref[step, plane, rows]
            other_ref[plane + 4, rows] = newer
            part = newer * image_ref[step, plane, rows]
            if start:
                sums_ref[0, plane, rows] = part
            else:
                sums_ref[0, plane, rows] = sums_ref[0, plane, rows] + part
                part = firsts[0] * first_ref[step + 1, 0, plane, rows]
                part = part + firsts[1] * first_ref[step + 1, 1, plane, rows]
                part = part + firsts[2] * first_ref[step + 1, 2, plane, rows]
                sums_ref[1, plane, rows] = sums_ref[1, plane, rows] + part

        run(now_ref, body)

    backward(STEPS - 1, adj_ref.at[1], adj_ref.at[0], True)

    def backward_pair(pair, carry):
        backward(STEPS - 2 - 2 * pair, adj_ref.at[0], adj_ref.at[1], False)
        backward(STEPS - 3 - 2 * pair, adj_ref.at[1], adj_ref.at[0], False)
        return carry

    lax.fori_loop(0, STEPS // 2 - 1, backward_pair, 0)
    backward(0, adj_ref.at[0], adj_ref.at[1], False)

    def last(plane, rows, centre, second, *firsts):
        part = sums_ref[1, plane, rows]
        for axis in range(3):
            part = part + firsts[axis] * first_ref[0, axis, plane, rows]
        sums_ref[1, plane, rows] = part * speed_ref[plane, rows]

    run(adj_ref.at[1], last)

    def code(route, index):
        plane = chunk_of(route, index, y)
        for field in range(2):
            values = [
                sums_ref[field, block * B + plane, 8 * route : 8 * route + 8] for block in range(APX)
            ]
            largest = jnp.abs(values[0])
            for value in values[1:]:
                largest = jnp.maximum(largest, jnp.abs(value))
            largest = jnp.maximum(jnp.max(largest, axis=(0, 1), keepdims=True), SMALLEST)
            units_ref[route, index, field : field + 1] = jnp.broadcast_to(largest * (1.0 / LEVELS), (1, NZ))
            levels = LEVELS / largest
            for pair in range(APX // 2):
                both = jnp.concatenate(values[2 * pair : 2 * pair + 2], axis=0)
                grads_ref[route, index, field, pair] = to_levels(both * levels)

    def grad_copy(route, by):
        target = shifted(mine[route], by, shots)
        return remote(
            grads_ref.at[route, target], grads_all.at[route, mine[route]],
            grad_send.at[route, by], grad_recv.at[route, by], on_route(route, target),
        )

    def unit_copy(route, by):
        target = shifted(mine[route], by, shots)
        return remote(
            units_ref.at[route, target], units_all.at[route, mine[route]],
            unit_send.at[route, by], unit_recv.at[route, by], on_route(route, target),
        )

    def start_grad(i, carry):
        by = near_first(shots - i, shots)
        for route in range(2):
            code(route, shifted(mine[route], by, shots))
            grad_copy(route, by).start()
            unit_copy(route, by).start()
        return carry

    lax.fori_loop(1, shots, start_grad, 0)
    for route in range(2):
        code(route, mine[route])
        grads_all[route, mine[route]] = grads_ref[route, mine[route]]
        units_all[route, mine[route]] = units_ref[route, mine[route]]

    def spread(route, by):
        sender = shifted(mine[route], shots - by, shots)
        for field in range(2):
            unit = units_all[route, sender, field : field + 1]
            for pair in range(APX // 2):
                values = grads_all[route, sender, field, pair].astype(F32) * unit
                turned = [turn(values[8 * i : 8 * i + 8], lane_block) for i in range(2)]
                high, low = split_two(jnp.concatenate(turned, axis=0))
                rows = pl.ds(pl.multiple_of(sender * positions + pair * 16, 16), 16)
                spread_ref[route, 0, rows, field * NZ : field * NZ + NZ] = high
                spread_ref[route, 1, rows, field * NZ : field * NZ + NZ] = low

    block = depths * owned

    def gx_copy(route, along):
        target = shifted(x, along, across)
        return remote(
            whole_levels.at[route, rows_at(target * block, block)], from_x.at[route, along],
            gx_send.at[route, along], gx_recv.at[route, along], (mine[0], target * depths + z),
        )

    def gx_lines(route, along):
        target = shifted(x, along, across)
        return remote(
            whole_lines.at[route, target], lines_x.at[route, along],
            xu_send.at[route, along], xu_recv.at[route, along], (mine[0], target * depths + z),
        )

    def merge(route, along):
        target = shifted(x, along, across)
        rows = rows_at(target * block, block)
        parts = spread_ref[route].reshape(2 * shots * positions, 2 * NZ)
        added = jnp.dot(place_ref[route, rows], parts, preferred_element_type=F32)
        if along == 0:
            column[route] = added
            return
        coded, units = row_levels(added)
        whole_levels[route, rows] = coded
        whole_lines[route, target] = units
        gx_copy(route, along).start()
        gx_lines(route, along).start()

    for route in range(2):
        spread(route, 0)
    for route in range(2):

        def returned(i, carry):
            by = near_first(i, shots)
            grad_copy(route, by).wait_recv()
            unit_copy(route, by).wait_recv()
            spread(route, by)
            return carry

        lax.fori_loop(1, shots, returned, 0)
        for along in (2, 1, 3):
            merge(route, along)
    for route in range(2):
        merge(route, 0)

    def sum_x(route):
        summed = column[route]
        for along in (1, 3, 2):
            gx_copy(route, along).wait_recv()
            gx_lines(route, along).wait_recv()
            summed = summed + from_levels(from_x[route, along], jnp.transpose(lines_x[route, along]))
        column[route] = summed

    home = lax.rem(3 * y + z, depths)

    def gz_copy(by):
        target = shifted(z, by, depths)
        return remote(
            column.at[0, rows_at(target * owned, owned)], from_z.at[0, by],
            gz_send.at[0, by], gz_recv.at[0, by], (mine[0], x * depths + target),
        )

    def gy_copy(by):
        target = shifted(z, by, depths)
        return remote(
            column.at[1, rows_at(target * owned, owned)], from_z.at[1, y],
            gz_send.at[1, by], gz_recv.at[1, y], (home * 2 + core, x * depths + target),
        )

    def gy_arrival(from_y):
        return remote(
            column.at[1, rows_at(z * owned, owned)], from_z.at[1, from_y],
            gz_send.at[1, 0], gz_recv.at[1, from_y], (home * 2 + core, x * depths + shifted(z, 1, depths)),
        )

    def start_gz(by, carry):
        gz_copy(by).start()
        return carry

    def start_gy(by, carry):
        gy_copy(by).start()
        return carry

    sum_x(0)
    lax.fori_loop(1, depths, start_gz, 0)
    sum_x(1)
    lax.fori_loop(1, depths, start_gy, 0)

    @pl.when(home != y)
    def _():
        gy_copy(0).start()

    from_z[0, 0] = column[0, rows_at(z * owned, owned)]

    @pl.when(home == y)
    def _():
        from_z[1, y] = column[1, rows_at(z * owned, owned)]

    def end_z(by, carry):
        gz_copy(by).wait_recv()
        return carry

    def end_y(from_y, carry):
        @pl.when(jnp.logical_or(from_y != y, home != y))
        def _():
            gy_arrival(from_y).wait_recv()

        return carry

    lax.fori_loop(1, depths, end_z, 0)
    lax.fori_loop(0, depths, end_y, 0)
    for route in range(2):
        ended = from_z[route, 0]
        for by in range(1, depths):
            ended = ended + from_z[route, by]
        for field in range(2):
            out_ref[:, field, route * NZ : route * NZ + NZ] = ended[:, field * NZ : field * NZ + NZ]

    def finish_shots(by, carry):
        for route in range(2):
            shot_copy(route, by).wait_send()
            name_copy(route, by).wait_send()
            grad_copy(route, by).wait_send()
            unit_copy(route, by).wait_send()
        return carry

    def finish_z(by, carry):
        z_copy(by).wait_send()
        gz_copy(by).wait_send()
        gy_copy(by).wait_send()
        return carry

    lax.fori_loop(1, shots, finish_shots, 0)
    lax.fori_loop(1, depths, finish_z, 0)
    for route in range(2):
        for along in range(1, across):
            x_copy(route, along).wait_send()
            gx_copy(route, along).wait_send()
            gx_lines(route, along).wait_send()

    @pl.when(home != y)
    def _():
        gy_copy(0).wait_send()


def shot_gradients(tile_store, aperture, model, source, pulses, cells, traces, fwd, adj, shots, tiles):
    vmem = pl.BlockSpec(memory_space=pltpu.VMEM)
    smem = pl.BlockSpec(memory_space=pltpu.SMEM)
    hbm = pl.BlockSpec(memory_space=pltpu.HBM)
    owned = model.shape[0]
    lanes = model.shape[1] // shots
    depths = DEPTH_CHIPS
    across = tiles // depths
    total = tiles * owned
    positions = APX * APZ
    groups = shots * positions // NZ
    rows = depths * owned
    volume = (NX, NY, NZ)
    padded = (NX + 8, NY, NZ)
    int16 = jnp.int16
    dma = pltpu.SemaphoreType.DMA
    depth, middle = depth_matrix(), middle_matrix()
    return pl.pallas_call(
        shot_kernel,
        out_shape=jax.ShapeDtypeStruct((owned, 2, lanes // 2), F32),
        in_specs=[vmem, vmem, vmem, smem, smem, vmem, vmem, hbm, hbm, hbm, hbm],
        out_specs=vmem,
        scratch_shapes=[
            pltpu.VMEM(depth.shape, BF16),
            pltpu.VMEM(middle.shape, BF16),
            pltpu.VMEM(depth.shape, F32),
            pltpu.VMEM(middle.shape, F32),
            dma((6,)),
            pltpu.VMEM((depths, 2, owned, 2 * NZ), BF16),
            pltpu.VMEM((8, NZ), F32),
            pltpu.VMEM((tiles, 2, owned, 2 * NZ), BF16),
            pltpu.VMEM((2, shots * positions, total), BF16),
            pltpu.VMEM((2, shots, 8, NZ), F32),
            pltpu.VMEM((2, shots, positions, 2 * NZ), BF16),
            pltpu.VMEM((2, shots, positions, 2 * NZ), BF16),
            pltpu.VMEM(padded, F32),
            pltpu.VMEM(volume, F32),
            pltpu.VMEM((3,) + volume, F32),
            pltpu.VMEM((2,) + padded, F32),
            pltpu.VMEM((2,) + padded, F32),
            pltpu.VMEM((STEPS,) + volume, F32),
            pltpu.VMEM((STEPS, 3) + volume, F32),
            pltpu.VMEM((STEPS,) + volume, F32),
            pltpu.VMEM((NX * NY, NREC), BF16),
            pltpu.VMEM(volume, F32),
            pltpu.VMEM((2,) + volume, F32),
            pltpu.VMEM((2, B, 2, APX // 2, 16, NZ), int16),
            pltpu.VMEM((2, B, 2, NZ), F32),
            pltpu.VMEM((2, shots, 2, APX // 2, 16, NZ), int16),
            pltpu.VMEM((2, shots, 2, NZ), F32),
            pltpu.VMEM((2, total, 2 * groups * NZ), BF16),
            pltpu.VMEM((2, 2, shots * positions, 2 * NZ), BF16),
            pltpu.VMEM((2, total, 2 * NZ), int16),
            pltpu.VMEM((2, across, 8, rows), F32),
            pltpu.VMEM((2, across, rows, 2 * NZ), int16),
            pltpu.VMEM((2, across, 8, rows), F32),
            pltpu.VMEM((2, rows, 2 * NZ), F32),
            pltpu.VMEM((2, depths, owned, 2 * NZ), F32),
            dma((depths,)), dma((depths,)),
            dma((2, across)), dma((2, across)),
            dma((2, shots)), dma((2, shots)), dma((2, shots)), dma((2, shots)),
            dma((2, shots)), dma((2, shots)), dma((2, shots)), dma((2, shots)),
            dma((2, across)), dma((2, across)), dma((2, across)), dma((2, across)),
            dma((2, depths)), dma((2, depths)),
        ],
        compiler_params=pltpu.CompilerParams(
            collective_id=0, has_side_effects=True, vmem_limit_bytes=56 * 1024 * 1024
        ),
        cost_estimate=pl.CostEstimate(flops=2 * 10**9, bytes_accessed=5 * 2**20, transcendentals=0),
        name="shot_gradients",
    )(
        tile_store, aperture, model, source, pulses, cells, traces, fwd, adj,
        jnp.asarray(depth.astype(np.float32)), jnp.asarray(middle.astype(np.float32)),
    )


def per_device(
    tile_store, apertures, model, fwd_states, adj_states, source_cell, wavelet, receiver_cells, residuals
):
    shots, tiles = lax.axis_size("shot"), lax.axis_size("tile")
    owned = model.shape[0]
    return shot_gradients(
        tile_store.reshape(1, -1), apertures, model.reshape(owned, -1), source_cell, wavelet,
        receiver_cells, residuals[0], fwd_states, adj_states, shots, tiles,
    )


def solution(mesh):
    return jax.shard_map(
        per_device,
        mesh=mesh,
        in_specs=(
            P(),
            P(("shot", "tile"), None),
            P("tile", None, None),
            P(("shot", "tile"), None, None, None, None),
            P(("shot", "tile"), None, None, None, None),
            P(("shot", "tile")),
            P(("shot", "tile"), None),
            P(("shot", "tile"), None),
            P(("shot", "tile"), None, None),
        ),
        out_specs=P("tile", None, "shot"),
        check_vma=False,
    )
```
